256 devices in a mesh: row: 128 (over x, y, z), col: 2 (over core).
Axes of the slice: x: 4, y: 4, z: 8, core: 2. Of those that a mesh axis runs over, the one named last changes fastest.
Arguments:
- inv_diag: float32 [128, 1088, 1088], P('row', None, 'col'), may hold values from -0.1875 to 0.1875
- low_left: float32 [128, 1088, 96], P('row', 'col'), may hold values from -0.1875 to 0.1875
- low_right: float32 [128, 1088, 96], P('row', 'col'), may hold values from -0.625 to 0.625
- deriv_diag: bfloat16 [3, 128, 1088, 1088], P(None, 'row', None, 'col'), may hold values from -0.1875 to 0.1875
- deriv_left: float32 [3, 128, 1088, 96], P(None, 'row', 'col'), may hold values from -0.1875 to 0.1875
- deriv_right: float32 [3, 128, 1088, 96], P(None, 'row', 'col'), may hold values from -0.625 to 0.625
- ranks: int32 [4, 128], P(None, 'row'), may hold values from 88 to 96
- whitened: float32 [139264], P(('row', 'col')), may hold values from -6 to 6
- probes: int32 [8, 139264], P(None, ('row', 'col')), may hold values from -1 to 1, as said below
Outputs:
- solved: float32 [9, 139264], P(None, ('row', 'col'))
- whitened_deriv: float32 [3, 8, 139264], P(None, None, ('row', 'col'))
- fisher: float32 [3, 3], replicated
- score: float32 [3], replicated
The draws below stay inside these ranges and needn't reach their ends.
Inputs may be any that keep to these rules, and one draw needn't show every extreme that they name: `probes`: every entry is -1 or +1. `ranks`: column 0 belongs to no tile.
All inputs are finite; a program needn't handle non-finite values.
Results may differ from the reference program's by a relative error of at most 0.0019.
Values sent between devices are 32-bit elements; how exact they have to be, the bound alone decides.
No kernel may reach another device: no remote copies, remote signals or barrier semaphores. Data moves between devices by JAX's collectives and lax.ppermute only.
A program may use at most 64 MiB of HBM per device.

```python
import jax
import jax.numpy as jnp
from jax import lax

B = 1088
RMAX = 96
PROBES = 8
PARAMS = 3
NT = 128
NTOT = 139264


def draw_probes(key, part):
    bits = jax.random.randint(key, (PROBES, NTOT), 0, 2)
    return (2 * bits - 1).astype(jnp.int32)


def place_ends(drawn, key, smallest, high):
    longest = drawn.shape.index(max(drawn.shape))
    spots = []
    for shift in (0, 1):
        where = [jax.random.randint(jax.random.fold_in(key, axis), (), 0, length) for axis, length in enumerate(drawn.shape)]
        where[longest] = (where[longest] + shift) % drawn.shape[longest]
        spots.append(tuple(where))
    return drawn.at[spots[0]].set(smallest).at[spots[1]].set(high)


def block_levels(own_key, extent, cuts, low, top_value):
    def one(axis_at, blocks):
        heights = jax.random.uniform(jax.random.fold_in(jax.random.fold_in(own_key, 6), axis_at), (blocks,), jnp.float32, low / len(cuts), top_value / len(cuts))
        return jnp.repeat(jnp.exp(heights), extent[axis_at] // blocks).reshape((-1,) + (1,) * (len(extent) - axis_at - 1))

    factor_of = one(*cuts[0])
    for cut in cuts[1:]:
        factor_of = factor_of * one(*cut)
    return factor_of


def centred(rng, dims, scale, limit, cuts=(), held_as=jnp.bfloat16):
    array = jax.random.normal(rng, dims, jnp.float32) * scale
    if len(cuts) > 0:
        array = block_levels(rng, dims, cuts, -0.22, 0.18) * array
    return jnp.clip(array, min=-limit, max=limit).astype(held_as)


def setup_inputs(seed: int = 0) -> dict:
    splits = jax.random.split(jax.random.key(seed), 10)
    return {
        "inv_diag": centred(splits[0], (NT, B, B), B ** -0.5, 0.1875, ((0, 128), (2, 2)), jnp.float32),
        "low_left": centred(splits[1], (NT, B, RMAX), B ** -0.5, 0.1875, ((0, 128), (1, 2)), jnp.float32),
        "low_right": centred(splits[2], (NT, B, RMAX), (RMAX - 4) ** -0.5, 0.625, ((0, 128), (1, 2)), jnp.float32),
        "deriv_diag": centred(splits[3], (PARAMS, NT, B, B), B ** -0.5, 0.1875, ((1, 128), (3, 2))),
        "deriv_left": centred(splits[4], (PARAMS, NT, B, RMAX), B ** -0.5, 0.1875, ((1, 128), (2, 2)), jnp.float32),
        "deriv_right": centred(splits[5], (PARAMS, NT, B, RMAX), RMAX ** -0.5, 0.625, ((1, 128), (2, 2)), jnp.float32),
        "ranks": place_ends(jax.random.randint(splits[6], (PARAMS + 1, NT), RMAX - 8, RMAX + 1), jax.random.fold_in(splits[6], 1), RMAX - 8, RMAX).astype(jnp.int32),
        "whitened": centred(splits[7], (NTOT,), 1.0, 6.0, ((0, 256),), jnp.float32),
        "probes": draw_probes(jax.random.fold_in(splits[9], 71), 0),
    }


def reference(inv_diag, low_left, low_right, deriv_diag, deriv_left, deriv_right, ranks, whitened, probes):
    highest = lax.Precision.HIGHEST
    tiles, size, rmax = low_left.shape
    params = deriv_left.shape[0]
    count = probes.shape[0]
    total = tiles * size
    columns = jnp.arange(rmax, dtype=jnp.int32)
    masks = (columns[None, None, :] < ranks[:, :, None]).astype(jnp.float32)
    masked_right = low_right * masks[0][:, None, :]
    deriv_masked = deriv_right * masks[1:][:, :, None, :]
    source = jnp.concatenate([whitened[None, :], probes.astype(jnp.float32)], axis=0)
    source = source.reshape(count + 1, tiles, size).transpose(1, 0, 2)
    empty_factor = jnp.zeros((1, size, rmax), jnp.float32)
    next_left = jnp.concatenate([low_left[1:], empty_factor], 0)
    next_right = jnp.concatenate([masked_right[1:], empty_factor], 0)

    def backward(later, item):
        inverse, left, right, rows = item
        coeff = jnp.dot(later, left, precision=highest)
        rest = rows - jnp.dot(coeff, right.T, precision=highest)
        current = jnp.dot(rest, inverse, precision=highest)
        return current, current

    start = jnp.zeros((count + 1, size), jnp.float32)
    _, solved_tiles = lax.scan(backward, start, (inv_diag, next_left, next_right, source), reverse=True)

    rounded = solved_tiles.astype(jnp.bfloat16)

    def dense_one(index):
        block = lax.dynamic_index_in_dim(deriv_diag, index, 1, keepdims=False)
        rows = lax.dynamic_index_in_dim(rounded, index, 0, keepdims=False)
        return jnp.stack([jnp.dot(rows, block[k].T, preferred_element_type=jnp.float32) for k in range(params)])

    dense = lax.map(dense_one, jnp.arange(tiles, dtype=jnp.int32))
    zero_tile = jnp.zeros((1, count + 1, size), jnp.float32)
    prior = jnp.concatenate([zero_tile, solved_tiles[:-1]], 0)
    lower_coeff = jnp.einsum('tpb,ktbr->ktpr', prior, deriv_masked, precision=highest)
    lower = jnp.einsum('ktpr,ktbr->tkpb', lower_coeff, deriv_left, precision=highest)
    upper_coeff = jnp.einsum('tpb,ktbr->ktpr', solved_tiles, deriv_left, precision=highest)
    upper_here = jnp.einsum('ktpr,ktbr->tkpb', upper_coeff, deriv_masked, precision=highest)
    zero_block = jnp.zeros((1, params, count + 1, size), jnp.float32)
    upper = jnp.concatenate([upper_here[1:], zero_block], 0)
    applied = dense + lower + upper

    drive = applied[:, :, 1:].reshape(tiles, params * count, size)

    def forward(earlier, item):
        inverse, left, right, rows = item
        coeff = jnp.dot(earlier, right, precision=highest)
        rest = rows - jnp.dot(coeff, left.T, precision=highest)
        current = jnp.dot(rest, inverse.T, precision=highest)
        return current, current

    begin = jnp.zeros((params * count, size), jnp.float32)
    _, deriv_tiles = lax.scan(forward, begin, (inv_diag, low_left, masked_right, drive))
    four = deriv_tiles.reshape(tiles, params, count, size)
    solved = solved_tiles.transpose(1, 0, 2).reshape(count + 1, total)
    whitened_deriv = four.transpose(1, 2, 0, 3).reshape(params, count, total)
    trace = jnp.einsum('tkpb,tpb->k', four, source[:, 1:], precision=highest)
    fisher = jnp.einsum('tkpb,tlpb->kl', four, four, precision=highest) / (2.0 * count * total)
    data = jnp.einsum('tkb,tb->k', applied[:, :, 0], solved_tiles[:, 0], precision=highest)
    score = (data - trace / count) / (2.0 * total)
    return solved, whitened_deriv, fisher, score
```

```python
import jax
import jax.numpy as jnp
from jax import lax
from jax.sharding import Mesh
from jax.sharding import PartitionSpec as P

ROW = ("row_0", "row_1", "row_2")
PLANE = ("row_0", "row_1")
LINE = "row_2"
ROW_COL = ("row_0", "row_1", "row_2", "col")

high = lax.Precision.HIGH
highest = lax.Precision.HIGHEST


def dot(a, b, precision=highest):
    return lax.dot_general(a, b, (((1,), (0,)), ((), ())), precision=precision, preferred_element_type=jnp.float32)


def dot_nt(a, b, precision=highest):
    return lax.dot_general(a, b, (((1,), (1,)), ((), ())), precision=precision, preferred_element_type=jnp.float32)


def dot_tn(a, b, precision=highest):
    return lax.dot_general(a, b, (((0,), (0,)), ((), ())), precision=precision, preferred_element_type=jnp.float32)


def along_rows(block, distance):
    devices = range(lax.axis_size(ROW))
    route = [(i, i + distance) for i in devices if i + distance in devices]
    return lax.ppermute(block, ROW, route)


def swapped(block):
    return lax.ppermute(block, "col", [(0, 1), (1, 0)])


def part(x, index, axis):
    size = x.shape[axis] // 2
    return lax.dynamic_slice_in_dim(x, index * size, size, axis)


def joined(mine, other, side, axis):
    first = jnp.where(side == 0, mine, other)
    second = jnp.where(side == 0, other, mine)
    return jnp.concatenate([first, second], axis)


def everywhere(x, axis):
    count = lax.axis_size(axis)
    return lax.all_to_all(jnp.broadcast_to(x[None], (count, *x.shape)), axis, 0, 0, tiled=True)


def body(
    inv_diag, low_left, low_right, deriv_diag, deriv_left, deriv_right, ranks, whitened, probes
):
    inverse = inv_diag[0]
    size, half = inverse.shape
    rmax = low_left.shape[2]
    count = probes.shape[0]
    params = deriv_left.shape[0]
    side = lax.axis_index("col")
    place = lax.axis_index(LINE)
    group = lax.axis_index(PLANE)
    in_line = lax.axis_size(LINE)
    groups = lax.axis_size(PLANE)
    right_next = along_rows(low_right[0], -1)
    columns = jnp.arange(rmax, dtype=jnp.int32)
    masks = (columns[None, :] < ranks[:, 0][:, None]).astype(jnp.float32)
    own_left = low_left[0] * masks[0][None, :]
    d_left = deriv_left[:, 0] * masks[1:][:, None, :]
    d_right = deriv_right[:, 0]
    source = jnp.concatenate([whitened[None, :], probes.astype(jnp.float32)], axis=0)
    source_other = swapped(source)
    source_full = joined(source, source_other, side, 1)
    moved = dot(inverse, own_left)
    moved = part(moved, side, 0) + swapped(part(moved, 1 - side, 0))
    lines = -(-(count + 1) // 16) * 16
    blank = jnp.zeros((lines - count - 1, rmax), jnp.float32)
    own_map = jnp.concatenate([-dot_tn(right_next, moved), dot(source, moved), blank], axis=0)
    own_map = part(own_map, side, 0) + swapped(part(own_map, 1 - side, 0))
    right_full = joined(right_next, swapped(right_next), side, 0)
    base = dot(source_full, inverse)
    wide = dot_tn(right_full, inverse)

    got = everywhere(own_map, LINE)
    maps = joined(got, swapped(got), side, 1)
    turns = maps[:, :rmax]
    lifts = maps[:, rmax:]
    reach = [None] * in_line
    reach[-1] = maps[-1]
    zero_top = jnp.zeros((rmax, rmax), jnp.float32)
    for k in reversed(range(in_line - 1)):
        reach[k] = dot(reach[k + 1], turns[k]) + jnp.concatenate([zero_top, lifts[k]], axis=0)
    total_map = reach[0]
    got = everywhere(part(total_map, side, 0), PLANE)
    totals = joined(got, swapped(got), side, 1)
    state = jnp.zeros((lines, rmax), jnp.float32)
    ahead = state
    for g in reversed(range(1, groups)):
        state = totals[g, rmax:] + dot(state, totals[g, :rmax])
        ahead = jnp.where(group == g - 1, state, ahead)
    coeff = ahead
    for k in range(1, in_line):
        through = reach[k][rmax:] + dot(ahead, reach[k][:rmax])
        coeff = jnp.where(place == k - 1, through, coeff)
    coeff = coeff[: count + 1]
    solution = base - dot(coeff, wide)

    rounded = solution.astype(jnp.bfloat16)
    prior = along_rows(solution, 1)
    upper_part = jnp.einsum("ph,khr->kpr", solution, d_left, precision=high)
    upper_coeff = upper_part + swapped(upper_part)
    upper_send = jnp.einsum("kpr,khr->kph", upper_coeff, d_right, precision=high)
    upper = along_rows(upper_send, -1)
    dense_part = jnp.einsum(
        "ph,kbh->kpb", rounded, deriv_diag[:, 0], preferred_element_type=jnp.float32
    )
    dense = part(dense_part, side, 2) + swapped(part(dense_part, 1 - side, 2))
    lower_part = jnp.einsum("ph,khr->kpr", prior, d_right, precision=high)
    lower_coeff = lower_part + swapped(lower_part)
    lower = jnp.einsum("kpr,khr->kph", lower_coeff, d_left, precision=high)
    applied = dense + lower + upper
    drive = applied[:, 1:].reshape(params * count, half)
    shared = dot_nt(drive, wide, high)
    shared = shared + swapped(shared)
    plain = dot_nt(drive, inverse, high)
    plain = part(plain, side, 1) + swapped(part(plain, 1 - side, 1))

    offsets = everywhere(shared, LINE)
    state = jnp.zeros_like(shared)
    local = state
    spread = jnp.eye(rmax, dtype=jnp.float32)
    own_spread = spread
    for k in range(in_line):
        state = offsets[k] + dot_nt(state, turns[k], high)
        if k < in_line - 1:
            spread = dot_nt(spread, turns[k], high) if k else turns[0].T
            local = jnp.where(place == k + 1, state, local)
            own_spread = jnp.where(place == k + 1, spread, own_spread)
    outs = everywhere(state, PLANE)
    state = jnp.zeros_like(shared)
    behind = state
    for g in range(groups - 1):
        state = outs[g] + dot_nt(state, totals[g, :rmax], high)
        behind = jnp.where(group == g + 1, state, behind)
    entry = local + dot(behind, own_spread, high)
    flat_result = plain - dot_nt(entry, moved, high)
    result = flat_result.reshape(params, count, half)

    trace_part = jnp.einsum("kph,ph->k", result, source[1:], precision=high)
    fisher_part = jnp.einsum("kph,lph->kl", result, result, precision=high)
    data_part = jnp.einsum("kh,h->k", applied[:, 0], solution[0], precision=high)
    sums = jnp.concatenate(
        [fisher_part.reshape(-1), trace_part, data_part, jnp.zeros((128 - params * (params + 2),))]
    )
    sums = sums + swapped(sums)
    sums = jnp.sum(everywhere(sums, ROW).reshape(-1, 128), axis=0)
    fisher_sum = sums[: params * params].reshape(params, params)
    trace = sums[params * params : params * (params + 1)]
    data = sums[params * (params + 1) : params * (params + 2)]
    total = lax.axis_size(ROW) * lax.axis_size("col") * half
    fisher = fisher_sum / (2.0 * count * total)
    score = (data - trace / count) / (2.0 * total)
    return (solution, result, fisher, score)


def solution(mesh):
    finer = Mesh(
        mesh.devices.reshape(4, 4, 8, mesh.shape["col"]), ("row_0", "row_1", "row_2", "col")
    )
    placed = (
        P(ROW, None, "col"),
        P(ROW, "col", None),
        P(ROW, "col", None),
        P(None, ROW, None, "col"),
        P(None, ROW, "col", None),
        P(None, ROW, "col", None),
        P(None, ROW),
        P(ROW_COL),
        P(None, ROW_COL),
    )
    return jax.shard_map(
        body,
        mesh=finer,
        in_specs=placed,
        out_specs=(P(None, ROW_COL), P(None, None, ROW_COL), P(), P()),
        check_vma=False,
    )
```

```python
import functools

import jax
import jax.numpy as jnp
from jax import lax
from jax.experimental import pallas as pl
from jax.experimental.pallas import tpu as pltpu
from jax.sharding import Mesh
from jax.sharding import PartitionSpec as P

ROW = ("row_0", "row_1", "row_2")
PLANE = ("row_0", "row_1")
LINE = "row_2"
ROW_COL = ("row_0", "row_1", "row_2", "col")

high = lax.Precision.HIGH
highest = lax.Precision.HIGHEST


def dot(a, b, precision=highest):
    return lax.dot_general(a, b, (((1,), (0,)), ((), ())), precision=precision, preferred_element_type=jnp.float32)


def dot_nt(a, b, precision=highest):
    return lax.dot_general(a, b, (((1,), (1,)), ((), ())), precision=precision, preferred_element_type=jnp.float32)


def dot_tn(a, b, precision=highest):
    return lax.dot_general(a, b, (((0,), (0,)), ((), ())), precision=precision, preferred_element_type=jnp.float32)


def along_rows(block, distance):
    devices = range(lax.axis_size(ROW))
    route = [(i, i + distance) for i in devices if i + distance in devices]
    return lax.ppermute(block, ROW, route)


def swapped(block):
    return lax.ppermute(block, "col", [(0, 1), (1, 0)])


def part(x, index, axis):
    size = x.shape[axis] // 2
    return lax.dynamic_slice_in_dim(x, index * size, size, axis)


def joined(mine, other, side, axis):
    first = jnp.where(side == 0, mine, other)
    second = jnp.where(side == 0, other, mine)
    return jnp.concatenate([first, second], axis)


def everywhere(x, axis):
    count = lax.axis_size(axis)
    return lax.all_to_all(jnp.broadcast_to(x[None], (count, *x.shape)), axis, 0, 0, tiled=True)


LANES = 128
SMEM = pl.BlockSpec(memory_space=pltpu.SMEM)
VMEM = pl.BlockSpec(memory_space=pltpu.VMEM)


def on_core(kernel, outs, scalars, arrays, flops):
    moved = sum(a.size * a.dtype.itemsize for a in arrays) + sum(4 * o.size for o in outs)
    return pl.pallas_call(
        kernel,
        out_shape=outs,
        in_specs=[SMEM] + [VMEM] * len(arrays),
        out_specs=[VMEM] * len(outs),
        compiler_params=pltpu.CompilerParams(vmem_limit_bytes=40 * 1024 * 1024),
        cost_estimate=pl.CostEstimate(flops=flops, bytes_accessed=moved, transcendentals=0),
    )(scalars, *arrays)


def floats(*shape):
    return jax.ShapeDtypeStruct(shape, jnp.float32)


def whole_map(side, mine, other, k):
    first = jnp.where(side == 0, mine[k], other[k])
    second = jnp.where(side == 0, other[k], mine[k])
    return jnp.concatenate([first, second], axis=0)


def line_back(rmax, where, mine, other, reach, prefix, send):
    side, place = where[0], where[1]
    count, half_rows = mine.shape[0], mine.shape[1]
    rows = 2 * half_rows
    maps = [whole_map(side, mine, other, k) for k in range(count)]
    run = maps[-1]
    reach[count - 1] = run
    row = lax.broadcasted_iota(jnp.int32, (rmax, LANES), 0)
    lane = lax.broadcasted_iota(jnp.int32, (rmax, LANES), 1)
    early = (row == lane).astype(jnp.float32)
    chosen = early
    for k in range(count - 1):
        run = dot(run[:, :rows], maps[count - 2 - k])
        reach[count - 2 - k] = run
        early = maps[0][:rmax] if k == 0 else dot(maps[k][:rmax, :rmax], early)
        chosen = jnp.where(place == k + 1, early, chosen)
    prefix[...] = chosen
    out = jnp.where(side == 0, run[:half_rows], run[half_rows:])
    for g in range(send.shape[0]):
        send[g] = out


def plane_back(rmax, where, mine, other, reach, base, wide, solution):
    side, place, group = where[0], where[1], where[2]
    groups, half_rows = mine.shape[0], mine.shape[1]
    count = reach.shape[0]
    rows = 2 * half_rows
    row = lax.broadcasted_iota(jnp.int32, (rows - rmax, LANES), 0)
    lane = lax.broadcasted_iota(jnp.int32, (rows - rmax, LANES), 1)
    state = ((row + rmax == lane) & (row < base.shape[0])).astype(jnp.float32)
    ahead = state
    for g in reversed(range(1, groups)):
        state = dot(state[:, :rows], whole_map(side, mine, other, g))
        ahead = jnp.where(group == g - 1, state, ahead)
    through = dot(ahead[:, :rows], reach[jnp.minimum(place + 1, count - 1)])
    coeff = jnp.where(place == count - 1, ahead, through)
    change = dot(coeff[:, :rmax], wide[...])
    solution[...] = base[...] - change[: base.shape[0]]


def line_forward(rmax, where, mine, other, offsets, local, send):
    side, place = where[0], where[1]
    state = jnp.zeros(local.shape, jnp.float32)
    chosen = state
    for k in range(mine.shape[0]):
        chosen = jnp.where(place == k, state, chosen)
        turn = whole_map(side, mine, other, k)[:rmax, :rmax]
        state = offsets[k] + dot_nt(state, turn)
    local[...] = chosen
    for g in range(send.shape[0]):
        send[g] = state


def plane_forward(
    rmax, where, mine, other, outs, prefix, local, plain, moved, source, result, sums
):
    side, group = where[0], where[2]
    params = plain.shape[0] // (source.shape[0] - 1)
    state = jnp.zeros(local.shape, jnp.float32)
    behind = state
    for g in range(mine.shape[0] - 1):
        turn = whole_map(side, mine, other, g)[:rmax, :rmax]
        state = outs[g] + dot_nt(state, turn)
        behind = jnp.where(group == g + 1, state, behind)
    entry = local[...] + dot_nt(behind, prefix[:, :rmax])
    final = plain[...] - dot_nt(entry, moved[:, :rmax])
    result[...] = final
    each = final.shape[0] // params
    parts = [final[k * each : (k + 1) * each] for k in range(params)]
    signs = source[1:]
    lane = lax.broadcasted_iota(jnp.int32, sums.shape, 1)
    total = jnp.zeros(sums.shape, jnp.float32)
    for k in range(params):
        for j in range(k, params):
            both = jnp.sum(parts[k] * parts[j], keepdims=True)
            total = jnp.where((lane == k * params + j) | (lane == j * params + k), both, total)
        both = jnp.sum(parts[k] * signs, keepdims=True)
        total = jnp.where(lane == params * params + k, both, total)
    sums[...] = total


def body(
    inv_diag, low_left, low_right, deriv_diag, deriv_left, deriv_right, ranks, whitened, probes
):
    inverse = inv_diag[0]
    size, half = inverse.shape
    rmax = low_left.shape[2]
    count = probes.shape[0]
    params = deriv_left.shape[0]
    side = lax.axis_index("col")
    place = lax.axis_index(LINE)
    group = lax.axis_index(PLANE)
    in_line = lax.axis_size(LINE)
    groups = lax.axis_size(PLANE)
    right_next = along_rows(low_right[0], -1)
    columns = jnp.arange(rmax, dtype=jnp.int32)
    masks = (columns[None, :] < ranks[:, 0][:, None]).astype(jnp.float32)
    own_left = jnp.pad(low_left[0] * masks[0][None, :], ((0, 0), (0, LANES - rmax)))
    where = jnp.stack([side, place, group]).astype(jnp.int32)
    d_left = deriv_left[:, 0] * masks[1:][:, None, :]
    d_right = deriv_right[:, 0]
    source = jnp.concatenate([whitened[None, :], probes.astype(jnp.float32)], axis=0)
    source_other = swapped(source)
    source_full = joined(source, source_other, side, 1)
    moved = dot(inverse, own_left)
    moved = part(moved, side, 0) + swapped(part(moved, 1 - side, 0))
    lines = -(-(count + 1) // 16) * 16
    blank = jnp.zeros((lines - count - 1, LANES), jnp.float32)
    keep = jnp.pad(jnp.eye(count + 1, dtype=jnp.float32), ((rmax, lines - count - 1), (rmax, LANES - rmax - count - 1)))
    own_map = jnp.concatenate([-dot_tn(right_next, moved), dot(source, moved), blank], axis=0)
    own_map = part(own_map, side, 0) + swapped(part(own_map, 1 - side, 0)) + part(keep, side, 0)
    right_full = joined(right_next, swapped(right_next), side, 0)
    base = dot(source_full, inverse)
    wide = dot_tn(right_full, inverse)

    rows = rmax + lines
    maps = everywhere(own_map, LINE)
    maps_other = swapped(maps)
    reach, prefix, send = on_core(
        functools.partial(line_back, rmax),
        [floats(in_line, rows, LANES), floats(rmax, LANES), floats(groups, rows // 2, LANES)],
        where,
        [maps, maps_other],
        4 * in_line * rows * rmax * rmax,
    )
    totals = lax.all_to_all(send, PLANE, 0, 0, tiled=True)
    totals_other = swapped(totals)
    (solution,) = on_core(
        functools.partial(plane_back, rmax),
        [floats(count + 1, half)],
        where,
        [totals, totals_other, reach, base, wide],
        2 * lines * rmax * (groups * LANES + half),
    )

    rounded = solution.astype(jnp.bfloat16)
    prior = along_rows(solution, 1)
    upper_part = jnp.einsum("ph,khr->kpr", solution, d_left, precision=high)
    upper_coeff = upper_part + swapped(upper_part)
    upper_send = jnp.einsum("kpr,khr->kph", upper_coeff, d_right, precision=high)
    upper = along_rows(upper_send, -1)
    dense_part = jnp.einsum(
        "ph,kbh->kpb", rounded, deriv_diag[:, 0], preferred_element_type=jnp.float32
    )
    dense = part(dense_part, side, 2) + swapped(part(dense_part, 1 - side, 2))
    lower_part = jnp.einsum("ph,khr->kpr", prior, d_right, precision=high)
    lower_coeff = lower_part + swapped(lower_part)
    lower = jnp.einsum("kpr,khr->kph", lower_coeff, d_left, precision=high)
    applied = dense + lower + upper
    drive = applied[:, 1:].reshape(params * count, half)
    shared = dot_nt(drive, wide, high)
    shared = shared + swapped(shared)
    plain = dot_nt(drive, inverse, high)
    plain = part(plain, side, 1) + swapped(part(plain, 1 - side, 1))

    data_part = jnp.einsum("kh,h->k", applied[:, 0], solution[0], precision=highest)
    offsets = everywhere(shared, LINE)
    local, send = on_core(
        functools.partial(line_forward, rmax),
        [floats(params * count, rmax), floats(groups, params * count, rmax)],
        where,
        [maps, maps_other, offsets],
        2 * in_line * params * count * rmax * rmax,
    )
    outs = lax.all_to_all(send, PLANE, 0, 0, tiled=True)
    flat_result, sums = on_core(
        functools.partial(plane_forward, rmax),
        [floats(params * count, half), floats(1, LANES)],
        where,
        [totals, totals_other, outs, prefix, local, plain, moved, source],
        2 * params * count * rmax * (groups * rmax + half),
    )
    result = flat_result.reshape(params, count, half)
    data_at = params * (params + 1)
    sums = sums.reshape(-1) + jnp.pad(data_part, (data_at, LANES - data_at - params))
    sums = sums + swapped(sums)
    sums = jnp.sum(everywhere(sums, ROW).reshape(-1, 128), axis=0)
    fisher_sum = sums[: params * params].reshape(params, params)
    trace = sums[params * params : params * (params + 1)]
    data = sums[params * (params + 1) : params * (params + 2)]
    total = lax.axis_size(ROW) * lax.axis_size("col") * half
    fisher = fisher_sum / (2.0 * count * total)
    score = (data - trace / count) / (2.0 * total)
    return (solution, result, fisher, score)


def solution(mesh):
    finer = Mesh(
        mesh.devices.reshape(4, 4, 8, mesh.shape["col"]), ("row_0", "row_1", "row_2", "col")
    )
    placed = (
        P(ROW, None, "col"),
        P(ROW, "col", None),
        P(ROW, "col", None),
        P(None, ROW, None, "col"),
        P(None, ROW, "col", None),
        P(None, ROW, "col", None),
        P(None, ROW),
        P(ROW_COL),
        P(None, ROW_COL),
    )
    return jax.shard_map(
        body,
        mesh=finer,
        in_specs=placed,
        out_specs=(P(None, ROW_COL), P(None, None, ROW_COL), P(), P()),
        check_vma=False,
    )
```

```python
import functools

import jax
import jax.numpy as jnp
from jax import lax
from jax.experimental import pallas as pl
from jax.experimental.pallas import tpu as pltpu
from jax.sharding import Mesh
from jax.sharding import PartitionSpec as P

ROW = ("row_0", "row_1", "row_2")
PLANE = ("row_0", "row_1")
LINE = "row_2"
ROW_COL = ("row_0", "row_1", "row_2", "col")

high = lax.Precision.HIGH
highest = lax.Precision.HIGHEST


def dot(a, b, precision=highest):
    return lax.dot_general(a, b, (((1,), (0,)), ((), ())), precision=precision, preferred_element_type=jnp.float32)


def dot_nt(a, b, precision=highest):
    return lax.dot_general(a, b, (((1,), (1,)), ((), ())), precision=precision, preferred_element_type=jnp.float32)


def dot_tn(a, b, precision=highest):
    return lax.dot_general(a, b, (((0,), (0,)), ((), ())), precision=precision, preferred_element_type=jnp.float32)


def along_rows(block, distance):
    devices = range(lax.axis_size(ROW))
    route = [(i, i + distance) for i in devices if i + distance in devices]
    return lax.ppermute(block, ROW, route)


def swapped(block):
    return lax.ppermute(block, "col", [(0, 1), (1, 0)])


def part(x, index, axis):
    size = x.shape[axis] // 2
    return lax.dynamic_slice_in_dim(x, index * size, size, axis)


def joined(mine, other, side, axis):
    first = jnp.where(side == 0, mine, other)
    second = jnp.where(side == 0, other, mine)
    return jnp.concatenate([first, second], axis)


def everywhere(x, axis):
    count = lax.axis_size(axis)
    return lax.all_to_all(jnp.broadcast_to(x[None], (count, *x.shape)), axis, 0, 0, tiled=True)


LANES = 128
SMEM = pl.BlockSpec(memory_space=pltpu.SMEM)
VMEM = pl.BlockSpec(memory_space=pltpu.VMEM)


def on_core(kernel, outs, scalars, arrays, flops, far=(), scratch=(), limit=40):
    moved = sum(a.size * a.dtype.itemsize for a in [*arrays, *far]) + sum(4 * o.size for o in outs)
    return pl.pallas_call(
        kernel,
        out_shape=outs,
        in_specs=[SMEM] + [VMEM] * len(arrays) + [pl.BlockSpec(memory_space=pl.ANY)] * len(far),
        out_specs=[VMEM] * len(outs),
        scratch_shapes=list(scratch),
        compiler_params=pltpu.CompilerParams(vmem_limit_bytes=limit * 1024 * 1024),
        cost_estimate=pl.CostEstimate(flops=flops, bytes_accessed=moved, transcendentals=0),
    )(scalars, *arrays, *far)


def floats(*shape):
    return jax.ShapeDtypeStruct(shape, jnp.float32)


def whole_map(side, mine, other, k):
    first = jnp.where(side == 0, mine[k], other[k])
    second = jnp.where(side == 0, other[k], mine[k])
    return jnp.concatenate([first, second], axis=0)


def line_back(rmax, where, mine, other, reach, prefix, send):
    side, place = where[0], where[1]
    count, half_rows = mine.shape[0], mine.shape[1]
    rows = 2 * half_rows
    maps = [whole_map(side, mine, other, k) for k in range(count)]
    run = maps[-1]
    reach[count - 1] = run
    row = lax.broadcasted_iota(jnp.int32, (rmax, LANES), 0)
    lane = lax.broadcasted_iota(jnp.int32, (rmax, LANES), 1)
    early = (row == lane).astype(jnp.float32)
    chosen = early
    for k in range(count - 1):
        run = dot(run[:, :rows], maps[count - 2 - k])
        reach[count - 2 - k] = run
        early = maps[0][:rmax] if k == 0 else dot(maps[k][:rmax, :rmax], early)
        chosen = jnp.where(place == k + 1, early, chosen)
    prefix[...] = chosen
    out = jnp.where(side == 0, run[:half_rows], run[half_rows:])
    for g in range(send.shape[0]):
        send[g] = out


def in_pieces(x, count):
    pieces = []
    for _ in range(count):
        piece = x.astype(jnp.bfloat16).astype(jnp.float32)
        pieces.append(piece)
        x = x - piece
    return pieces


def by_pieces(a, b, count, dims):
    rows = a.shape[0]
    stacked = jnp.concatenate(in_pieces(a, count), axis=0).astype(jnp.bfloat16)
    total = None
    for k, piece in enumerate(in_pieces(b, count)):
        product = lax.dot_general(
            stacked, piece.astype(jnp.bfloat16), (dims, ((), ())), preferred_element_type=jnp.float32
        )
        for j in reversed(range(count - k)):
            term = product[j * rows : (j + 1) * rows]
            total = term if total is None else total + term
    return total


def exact(a, b):
    return by_pieces(a, b, 3, ((1,), (0,)))


def close_nt(a, b):
    return by_pieces(a, b, 2, ((1,), (1,)))


def left_products(where, inverse, left, mine, other):
    half = left.shape[1]
    row = lax.broadcasted_iota(jnp.int32, left.shape, 0)
    product = dot(jnp.where(row < where[3], left[...], 0.0), inverse[...])
    first, second = product[:, :half], product[:, half:]
    mine[...] = jnp.where(where[0] == 0, first, second)
    other[...] = jnp.where(where[0] == 0, second, first)


def coupled(where, right, right_other, source, source_other, moved, moved_other, mine, other):
    rmax = right.shape[0]
    half_rows = mine.shape[0]
    vectors = source.shape[0]
    top = -(dot_nt(right[...], moved[...]) + dot_nt(right_other[...], moved_other[...]))
    low = dot_nt(source[...], moved[...]) + dot_nt(source_other[...], moved_other[...])
    low = jnp.concatenate([low, jnp.zeros((2 * half_rows - rmax - vectors, rmax), jnp.float32)], axis=0)
    full = jnp.concatenate([top, low], axis=0)
    full = jnp.concatenate([full, jnp.zeros((2 * half_rows, LANES - rmax), jnp.float32)], axis=1)
    row = lax.broadcasted_iota(jnp.int32, full.shape, 0)
    lane = lax.broadcasted_iota(jnp.int32, full.shape, 1)
    keep = (row == lane) & (row >= rmax) & (row < rmax + vectors)
    full = full + jnp.where(keep, 0.5, 0.0)
    first, second = full[:half_rows], full[half_rows:]
    mine[...] = jnp.where(where[0] == 0, first, second)
    other[...] = jnp.where(where[0] == 0, second, first)


def tile_products(where, inverse, source, source_other, right, right_other, out):
    half = source.shape[1]
    blank = jnp.zeros((16 - source.shape[0], half), jnp.float32)
    mine = jnp.concatenate([source[...], blank, right[...]], axis=0)
    other = jnp.concatenate([source_other[...], blank, right_other[...]], axis=0)
    first = jnp.where(where[0] == 0, mine, other)
    second = jnp.where(where[0] == 0, other, mine)
    out[...] = dot_nt(first, inverse[:, :half]) + dot_nt(second, inverse[:, half:])


def plane_back(
    rmax, where, mine, other, reach, both, wide_other, ahead_terms, here_terms, left, right, deriv,
    solution, upper, dense, dense_other, terms, held, arrived,
):
    params = left.shape[0]
    fetch = pltpu.make_async_copy(deriv, held, arrived)
    fetch.start()
    side, place, group = where[0], where[1], where[2]
    groups, half_rows = mine.shape[0], mine.shape[1]
    count = reach.shape[0]
    rows = 2 * half_rows
    vectors = solution.shape[0]
    lines = rows - rmax
    row = lax.broadcasted_iota(jnp.int32, (lines, LANES), 0)
    lane = lax.broadcasted_iota(jnp.int32, (lines, LANES), 1)
    state = ((row + rmax == lane) & (row < vectors)).astype(jnp.float32)
    ahead = state
    for g in reversed(range(1, groups)):
        state = exact(state[:, :rows], whole_map(side, mine, other, g))
        ahead = jnp.where(group == g - 1, state, ahead)
    through = exact(ahead[:, :rows], reach[jnp.minimum(place + 1, count - 1)])
    coeff = jnp.where(place == count - 1, ahead, through)[:, :rmax]
    own = exact(ahead[:, :rows], reach[place])[:, :rmax]
    solved = (both[:lines] - dot(coeff, both[lines:]))[:vectors]
    solution[...] = jnp.concatenate([solved[vectors - 1 :], solved[: vectors - 1]], axis=0)
    column = lax.broadcasted_iota(jnp.int32, (lines, rmax), 1)
    for k in range(left.shape[0]):
        below = here_terms[k, :lines] - dot(coeff, here_terms[k, lines:])
        below = jnp.where(column < where[4 + k], below, 0.0)
        above = ahead_terms[k, :lines] - dot(own, ahead_terms[k, lines:])
        above = jnp.where(column < where[4 + k], above, 0.0)
        upper[k] = dot(below, right[k])[:vectors]
        dense[k] = dot(above, left[k])[:vectors]
        terms[params + k] = dot_nt(above, here_terms[k, lines:])[: vectors - 1]
        terms[2 * params + k] = dot_nt(below, ahead_terms[k, lines:])[: vectors - 1]
    fetch.wait()
    half = both.shape[1]
    rounded = jnp.concatenate([solved, jnp.zeros((lines - vectors, half), jnp.float32)], axis=0)
    rounded = rounded.astype(jnp.bfloat16)
    wide = both[lines:]
    for k in range(left.shape[0]):
        product = jnp.dot(rounded, held[k], preferred_element_type=jnp.float32)
        first, second = product[:, :half], product[:, half:]
        here = jnp.where(side == 0, first, second)
        there = jnp.where(side == 0, second, first)
        dense[k] += here[:vectors]
        dense_other[k] = there[:vectors]
        terms[k] = (dot_nt(here, wide) + dot_nt(there, wide_other[...]))[: vectors - 1]


def line_forward(rmax, where, mine, other, offsets, local, send):
    side, place = where[0], where[1]
    state = jnp.zeros(local.shape, jnp.float32)
    chosen = state
    for k in range(mine.shape[0]):
        chosen = jnp.where(place == k, state, chosen)
        turn = whole_map(side, mine, other, k)[:rmax, :rmax]
        offset = offsets[k, : local.shape[0]]
        if k + 1 < mine.shape[0]:
            offset += offsets[k + 1, local.shape[0] :]
        state = offset + close_nt(state, turn)
    local[...] = chosen
    for g in range(send.shape[0]):
        send[g, : local.shape[0]] = state
        send[g, local.shape[0] :] = offsets[0, local.shape[0] :]


def plane_forward(
    rmax, where, mine, other, outs, prefix, local, plain, moved, source, result, sums
):
    side, group = where[0], where[2]
    params = plain.shape[0] // (source.shape[0] - 1)
    state = jnp.zeros(local.shape, jnp.float32)
    behind = state
    for g in range(mine.shape[0] - 1):
        turn = whole_map(side, mine, other, g)[:rmax, :rmax]
        offset = outs[g, : local.shape[0]] + outs[g + 1, local.shape[0] :]
        state = offset + close_nt(state, turn)
        behind = jnp.where(group == g + 1, state, behind)
    entry = local[...] + dot_nt(behind, prefix[:, :rmax])
    final = plain[...] - dot(entry, moved[...])
    result[...] = final
    each = final.shape[0] // params
    parts = [final[k * each : (k + 1) * each] for k in range(params)]
    signs = source[: source.shape[0] - 1]
    lane = lax.broadcasted_iota(jnp.int32, sums.shape, 1)
    total = jnp.zeros(sums.shape, jnp.float32)
    for k in range(params):
        for j in range(k, params):
            both = jnp.sum(parts[k] * parts[j], keepdims=True)
            total = jnp.where((lane == k * params + j) | (lane == j * params + k), both, total)
        both = jnp.sum(parts[k] * signs, keepdims=True)
        total = jnp.where(lane == params * params + k, both, total)
    sums[...] = total


def body(
    inv_diag, low_left, low_right, deriv_diag, deriv_left, deriv_right, ranks, whitened, probes
):
    inverse = jnp.swapaxes(inv_diag[0], 0, 1)
    half, size = inverse.shape
    rmax = low_left.shape[2]
    count = probes.shape[0]
    params = deriv_left.shape[0]
    side = lax.axis_index("col")
    place = lax.axis_index(LINE)
    group = lax.axis_index(PLANE)
    in_line = lax.axis_size(LINE)
    groups = lax.axis_size(PLANE)
    d_left = jnp.swapaxes(deriv_left[:, 0], 1, 2)
    d_right = jnp.swapaxes(deriv_right[:, 0], 1, 2)
    d_diag = jnp.swapaxes(deriv_diag[:, 0], 1, 2)
    left = jnp.swapaxes(low_left[0], 0, 1)
    right = jnp.swapaxes(low_right[0], 0, 1)
    where = jnp.concatenate([jnp.stack([side, place, group]).astype(jnp.int32), ranks[:, 0]])
    source = jnp.concatenate([probes.astype(jnp.float32), whitened[None, :]], axis=0)
    lines = -(-(count + 1) // 16) * 16
    rows = rmax + lines
    source_other = swapped(source)
    right_next = along_rows(right, -1)
    moved, moved_other = on_core(
        left_products, [floats(rmax, half)] * 2, where, [inverse, left], 2 * size * half * rmax
    )
    right_next, moved, moved_other = lax.optimization_barrier((right_next, moved, moved_other))
    right_other = swapped(right_next)
    map_mine, map_other = on_core(
        coupled,
        [floats(rows // 2, LANES)] * 2,
        where,
        [right_next, right_other, source, source_other, moved, moved_other],
        2 * size * rows * rmax,
    )
    own_map = map_mine + swapped(map_other)
    moved = moved + swapped(moved_other)
    (both,) = on_core(
        tile_products,
        [floats(rmax + lines, half)],
        where,
        [inverse, source, source_other, right_next, right_other],
        2 * (rmax + lines) * size * half,
    )
    maps = everywhere(own_map, LINE)
    maps, both = lax.optimization_barrier((maps, both))
    maps_other = swapped(maps)
    both_before = along_rows(both, 1)
    both_other = swapped(both[lines:])
    here_terms = jnp.einsum("mh,krh->kmr", both, d_left, precision=highest)
    here_terms = here_terms + swapped(here_terms)
    ahead_terms = jnp.einsum("mh,krh->kmr", both_before, d_right, precision=highest)
    ahead_terms = ahead_terms + swapped(ahead_terms)
    reach, prefix, send = on_core(
        functools.partial(line_back, rmax),
        [floats(in_line, rows, LANES), floats(rmax, LANES), floats(groups, rows // 2, LANES)],
        where,
        [maps, maps_other],
        4 * in_line * rows * rmax * rmax,
    )
    totals = lax.all_to_all(send, PLANE, 0, 0, tiled=True)
    totals, here_terms, ahead_terms, moved, both_other = lax.optimization_barrier(
        (totals, here_terms, ahead_terms, moved, both_other)
    )
    totals_other = swapped(totals)
    solution, upper_send, dense, dense_other, terms = on_core(
        functools.partial(plane_back, rmax),
        [floats(count + 1, half)]
        + [floats(params, count + 1, half)] * 3
        + [floats(3 * params, count, rmax)],
        where,
        [totals, totals_other, reach, both, both_other, ahead_terms, here_terms, d_left, d_right],
        2 * lines * rmax * (groups * LANES + (2 * params + 1) * half),
        [d_diag],
        [pltpu.VMEM(d_diag.shape, d_diag.dtype), pltpu.SemaphoreType.DMA],
        60,
    )
    upper = along_rows(upper_send, -1)
    partial = terms[:params]
    shared = jnp.concatenate([partial + swapped(partial) + terms[params : 2 * params], terms[2 * params :]], axis=0)
    shared = shared.reshape(2 * params * count, rmax)
    offsets = everywhere(shared, LINE)
    dense = dense + swapped(dense_other)
    applied = dense + upper
    drive = applied[:, :count].reshape(params * count, half)
    plain = dot(drive, inverse, high)
    plain = part(plain, side, 1) + swapped(part(plain, 1 - side, 1))

    data_part = jnp.einsum("kh,h->k", applied[:, count], solution[0], precision=highest)
    local, send = on_core(
        functools.partial(line_forward, rmax),
        [floats(params * count, rmax), floats(groups, 2 * params * count, rmax)],
        where,
        [maps, maps_other, offsets],
        2 * in_line * params * count * rmax * rmax,
    )
    outs = lax.all_to_all(send, PLANE, 0, 0, tiled=True)
    flat_result, sums = on_core(
        functools.partial(plane_forward, rmax),
        [floats(params * count, half), floats(1, LANES)],
        where,
        [totals, totals_other, outs, prefix, local, plain, moved, source],
        2 * params * count * rmax * (groups * rmax + half),
    )
    result = flat_result.reshape(params, count, half)
    data_at = params * (params + 1)
    sums = sums.reshape(-1) + jnp.pad(data_part, (data_at, LANES - data_at - params))
    sums = sums + swapped(sums)
    sums = jnp.sum(everywhere(sums, ROW).reshape(-1, 128), axis=0)
    fisher_sum = sums[: params * params].reshape(params, params)
    trace = sums[params * params : params * (params + 1)]
    data = sums[params * (params + 1) : params * (params + 2)]
    total = lax.axis_size(ROW) * lax.axis_size("col") * half
    fisher = fisher_sum / (2.0 * count * total)
    score = (data - trace / count) / (2.0 * total)
    return (solution, result, fisher, score)


def solution(mesh):
    finer = Mesh(
        mesh.devices.reshape(4, 4, 8, mesh.shape["col"]), ("row_0", "row_1", "row_2", "col")
    )
    placed = (
        P(ROW, None, "col"),
        P(ROW, "col", None),
        P(ROW, "col", None),
        P(None, ROW, None, "col"),
        P(None, ROW, "col", None),
        P(None, ROW, "col", None),
        P(None, ROW),
        P(ROW_COL),
        P(None, ROW_COL),
    )
    return jax.shard_map(
        body,
        mesh=finer,
        in_specs=placed,
        out_specs=(P(None, ROW_COL), P(None, None, ROW_COL), P(), P()),
        check_vma=False,
    )
```

```python
import functools

import jax
import jax.numpy as jnp
from jax import lax
from jax.experimental import pallas as pl
from jax.experimental.pallas import tpu as pltpu
from jax.sharding import Mesh
from jax.sharding import PartitionSpec as P

ROW = ("row_0", "row_1", "row_2")
PLANE = ("row_0", "row_1")
LINE = "row_2"
ROW_COL = ("row_0", "row_1", "row_2", "col")

high = lax.Precision.HIGH
highest = lax.Precision.HIGHEST


def dot(a, b, precision=highest):
    return lax.dot_general(a, b, (((1,), (0,)), ((), ())), precision=precision, preferred_element_type=jnp.float32)


def dot_nt(a, b, precision=highest):
    return lax.dot_general(a, b, (((1,), (1,)), ((), ())), precision=precision, preferred_element_type=jnp.float32)


def dot_tn(a, b, precision=highest):
    return lax.dot_general(a, b, (((0,), (0,)), ((), ())), precision=precision, preferred_element_type=jnp.float32)


def along_rows(block, distance):
    devices = range(lax.axis_size(ROW))
    route = [(i, i + distance) for i in devices if i + distance in devices]
    return lax.ppermute(block, ROW, route)


def swapped(block):
    return lax.ppermute(block, "col", [(0, 1), (1, 0)])


def part(x, index, axis):
    size = x.shape[axis] // 2
    return lax.dynamic_slice_in_dim(x, index * size, size, axis)


def joined(mine, other, side, axis):
    first = jnp.where(side == 0, mine, other)
    second = jnp.where(side == 0, other, mine)
    return jnp.concatenate([first, second], axis)


def everywhere(x, axis):
    count = lax.axis_size(axis)
    return lax.all_to_all(jnp.broadcast_to(x[None], (count, *x.shape)), axis, 0, 0, tiled=True)


LANES = 128
SMEM = pl.BlockSpec(memory_space=pltpu.SMEM)
VMEM = pl.BlockSpec(memory_space=pltpu.VMEM)


def on_core(kernel, outs, scalars, arrays, flops, far=(), scratch=(), limit=40):
    moved = sum(a.size * a.dtype.itemsize for a in [*arrays, *far]) + sum(4 * o.size for o in outs)
    return pl.pallas_call(
        kernel,
        out_shape=outs,
        in_specs=[SMEM] + [VMEM] * len(arrays) + [pl.BlockSpec(memory_space=pl.ANY)] * len(far),
        out_specs=[VMEM] * len(outs),
        scratch_shapes=list(scratch),
        compiler_params=pltpu.CompilerParams(vmem_limit_bytes=limit * 1024 * 1024),
        cost_estimate=pl.CostEstimate(flops=flops, bytes_accessed=moved, transcendentals=0),
    )(scalars, *arrays, *far)


def floats(*shape):
    return jax.ShapeDtypeStruct(shape, jnp.float32)


def whole_map(side, mine, other, k):
    first = jnp.where(side == 0, mine[k], other[k])
    second = jnp.where(side == 0, other[k], mine[k])
    return jnp.concatenate([first, second], axis=0)


def line_back(rmax, where, mine, other, reach, prefix, send):
    side, place = where[0], where[1]
    count, half_rows = mine.shape[0], mine.shape[1]
    rows = 2 * half_rows
    maps = [whole_map(side, mine, other, k) for k in range(count)]
    run = maps[-1]
    reach[count - 1] = run
    row = lax.broadcasted_iota(jnp.int32, (rmax, LANES), 0)
    lane = lax.broadcasted_iota(jnp.int32, (rmax, LANES), 1)
    early = (row == lane).astype(jnp.float32)
    chosen = early
    for k in range(count - 1):
        run = dot(run[:, :rows], maps[count - 2 - k])
        reach[count - 2 - k] = run
        early = maps[0][:rmax] if k == 0 else dot(maps[k][:rmax, :rmax], early)
        chosen = jnp.where(place == k + 1, early, chosen)
    prefix[...] = chosen
    out = jnp.where(side == 0, run[:half_rows], run[half_rows:])
    for g in range(send.shape[0]):
        send[g] = out


def in_pieces(x, count):
    pieces = []
    for _ in range(count):
        piece = x.astype(jnp.bfloat16).astype(jnp.float32)
        pieces.append(piece)
        x = x - piece
    return pieces


def by_pieces(a, b, count, dims):
    rows = a.shape[0]
    stacked = jnp.concatenate(in_pieces(a, count), axis=0).astype(jnp.bfloat16)
    total = None
    for k, piece in enumerate(in_pieces(b, count)):
        product = lax.dot_general(
            stacked, piece.astype(jnp.bfloat16), (dims, ((), ())), preferred_element_type=jnp.float32
        )
        for j in reversed(range(count - k)):
            term = product[j * rows : (j + 1) * rows]
            total = term if total is None else total + term
    return total


def exact(a, b):
    return by_pieces(a, b, 3, ((1,), (0,)))


def close(a, b):
    return by_pieces(a, b, 2, ((1,), (0,)))


def close_nt(a, b):
    return by_pieces(a, b, 2, ((1,), (1,)))


def left_products(where, inverse, left, mine, other):
    half = left.shape[1]
    row = lax.broadcasted_iota(jnp.int32, left.shape, 0)
    product = dot(jnp.where(row < where[3], left[...], 0.0), inverse[...])
    first, second = product[:, :half], product[:, half:]
    mine[...] = jnp.where(where[0] == 0, first, second)
    other[...] = jnp.where(where[0] == 0, second, first)


def coupled(where, right, right_other, source, source_other, moved, moved_other, mine, other):
    rmax = right.shape[0]
    half_rows = mine.shape[0]
    vectors = source.shape[0]
    top = -(dot_nt(right[...], moved[...]) + dot_nt(right_other[...], moved_other[...]))
    low = dot_nt(source[...], moved[...]) + dot_nt(source_other[...], moved_other[...])
    low = jnp.concatenate([low, jnp.zeros((2 * half_rows - rmax - vectors, rmax), jnp.float32)], axis=0)
    full = jnp.concatenate([top, low], axis=0)
    full = jnp.concatenate([full, jnp.zeros((2 * half_rows, LANES - rmax), jnp.float32)], axis=1)
    row = lax.broadcasted_iota(jnp.int32, full.shape, 0)
    lane = lax.broadcasted_iota(jnp.int32, full.shape, 1)
    keep = (row == lane) & (row >= rmax) & (row < rmax + vectors)
    full = full + jnp.where(keep, 0.5, 0.0)
    first, second = full[:half_rows], full[half_rows:]
    mine[...] = jnp.where(where[0] == 0, first, second)
    other[...] = jnp.where(where[0] == 0, second, first)


def tile_products(where, inverse, source, source_other, right, right_other, out):
    half = source.shape[1]
    blank = jnp.zeros((16 - source.shape[0], half), jnp.float32)
    mine = jnp.concatenate([source[...], blank, right[...]], axis=0)
    other = jnp.concatenate([source_other[...], blank, right_other[...]], axis=0)
    first = jnp.where(where[0] == 0, mine, other)
    second = jnp.where(where[0] == 0, other, mine)
    out[...] = dot_nt(first, inverse[:, :half]) + dot_nt(second, inverse[:, half:])


def plane_back(
    rmax, where, mine, other, reach, both, wide_other, ahead_terms, here_terms, left, right, deriv,
    solution, upper, dense, dense_other, terms, held, arrived,
):
    params = left.shape[0]
    fetch = pltpu.make_async_copy(deriv, held, arrived)
    fetch.start()
    side, place, group = where[0], where[1], where[2]
    groups, half_rows = mine.shape[0], mine.shape[1]
    count = reach.shape[0]
    rows = 2 * half_rows
    vectors = solution.shape[0]
    lines = rows - rmax
    row = lax.broadcasted_iota(jnp.int32, (lines, LANES), 0)
    lane = lax.broadcasted_iota(jnp.int32, (lines, LANES), 1)
    state = ((row + rmax == lane) & (row < vectors)).astype(jnp.float32)
    ahead = state
    for g in reversed(range(1, groups)):
        state = exact(state[:, :rows], whole_map(side, mine, other, g))
        ahead = jnp.where(group == g - 1, state, ahead)
    through = exact(ahead[:, :rows], reach[jnp.minimum(place + 1, count - 1)])
    coeff = jnp.where(place == count - 1, ahead, through)[:, :rmax]
    own = exact(ahead[:, :rows], reach[place])[:, :rmax]
    solved = (both[:lines] - dot(coeff, both[lines:]))[:vectors]
    solution[...] = jnp.concatenate([solved[vectors - 1 :], solved[: vectors - 1]], axis=0)
    column = lax.broadcasted_iota(jnp.int32, (lines, rmax), 1)
    for k in range(left.shape[0]):
        below = here_terms[k, :lines] - close(coeff, here_terms[k, lines:])
        below = jnp.where(column < where[4 + k], below, 0.0)
        above = ahead_terms[k, :lines] - close(own, ahead_terms[k, lines:])
        above = jnp.where(column < where[4 + k], above, 0.0)
        upper[k] = close(below, right[k])[:vectors]
        dense[k] = close(above, left[k])[:vectors]
        terms[params + k] = close_nt(above, here_terms[k, lines:])[: vectors - 1]
        terms[2 * params + k] = close_nt(below, ahead_terms[k, lines:])[: vectors - 1]
    fetch.wait()
    half = both.shape[1]
    rounded = jnp.concatenate([solved, jnp.zeros((lines - vectors, half), jnp.float32)], axis=0)
    rounded = rounded.astype(jnp.bfloat16)
    wide = both[lines:]
    for k in range(left.shape[0]):
        product = jnp.dot(rounded, held[k], preferred_element_type=jnp.float32)
        first, second = product[:, :half], product[:, half:]
        here = jnp.where(side == 0, first, second)
        there = jnp.where(side == 0, second, first)
        dense[k] += here[:vectors]
        dense_other[k] = there[:vectors]
        terms[k] = (close_nt(here, wide) + close_nt(there, wide_other[...]))[: vectors - 1]


def line_forward(rmax, where, mine, other, offsets, local, send):
    side, place = where[0], where[1]
    state = jnp.zeros(local.shape, jnp.float32)
    chosen = state
    for k in range(mine.shape[0]):
        chosen = jnp.where(place == k, state, chosen)
        turn = whole_map(side, mine, other, k)[:rmax, :rmax]
        offset = offsets[k, : local.shape[0]]
        if k + 1 < mine.shape[0]:
            offset += offsets[k + 1, local.shape[0] :]
        state = offset + close_nt(state, turn)
    local[...] = chosen
    for g in range(send.shape[0]):
        send[g, : local.shape[0]] = state
        send[g, local.shape[0] :] = offsets[0, local.shape[0] :]


def plane_forward(
    rmax, where, mine, other, outs, prefix, local, plain, moved, source, result, sums
):
    side, group = where[0], where[2]
    params = plain.shape[0] // (source.shape[0] - 1)
    state = jnp.zeros(local.shape, jnp.float32)
    behind = state
    for g in range(mine.shape[0] - 1):
        turn = whole_map(side, mine, other, g)[:rmax, :rmax]
        offset = outs[g, : local.shape[0]] + outs[g + 1, local.shape[0] :]
        state = offset + close_nt(state, turn)
        behind = jnp.where(group == g + 1, state, behind)
    entry = local[...] + close_nt(behind, prefix[:, :rmax])
    final = plain[...] - close(entry, moved[...])
    result[...] = final
    each = final.shape[0] // params
    parts = [final[k * each : (k + 1) * each] for k in range(params)]
    signs = source[: source.shape[0] - 1]
    lane = lax.broadcasted_iota(jnp.int32, sums.shape, 1)
    total = jnp.zeros(sums.shape, jnp.float32)
    for k in range(params):
        for j in range(k, params):
            both = jnp.sum(parts[k] * parts[j], keepdims=True)
            total = jnp.where((lane == k * params + j) | (lane == j * params + k), both, total)
        both = jnp.sum(parts[k] * signs, keepdims=True)
        total = jnp.where(lane == params * params + k, both, total)
    sums[...] = total


def body(
    inv_diag, low_left, low_right, deriv_diag, deriv_left, deriv_right, ranks, whitened, probes
):
    inverse = jnp.swapaxes(inv_diag[0], 0, 1)
    half, size = inverse.shape
    rmax = low_left.shape[2]
    count = probes.shape[0]
    params = deriv_left.shape[0]
    side = lax.axis_index("col")
    place = lax.axis_index(LINE)
    group = lax.axis_index(PLANE)
    in_line = lax.axis_size(LINE)
    groups = lax.axis_size(PLANE)
    d_left = jnp.swapaxes(deriv_left[:, 0], 1, 2)
    d_right = jnp.swapaxes(deriv_right[:, 0], 1, 2)
    d_diag = jnp.swapaxes(deriv_diag[:, 0], 1, 2)
    left = jnp.swapaxes(low_left[0], 0, 1)
    right = jnp.swapaxes(low_right[0], 0, 1)
    where = jnp.concatenate([jnp.stack([side, place, group]).astype(jnp.int32), ranks[:, 0]])
    source = jnp.concatenate([probes.astype(jnp.float32), whitened[None, :]], axis=0)
    lines = -(-(count + 1) // 16) * 16
    rows = rmax + lines
    source_other = swapped(source)
    right_next = along_rows(right, -1)
    moved, moved_other = on_core(
        left_products, [floats(rmax, half)] * 2, where, [inverse, left], 2 * size * half * rmax
    )
    right_next, moved, moved_other = lax.optimization_barrier((right_next, moved, moved_other))
    right_other = swapped(right_next)
    map_mine, map_other = on_core(
        coupled,
        [floats(rows // 2, LANES)] * 2,
        where,
        [right_next, right_other, source, source_other, moved, moved_other],
        2 * size * rows * rmax,
    )
    own_map = map_mine + swapped(map_other)
    moved = moved + swapped(moved_other)
    (both,) = on_core(
        tile_products,
        [floats(rmax + lines, half)],
        where,
        [inverse, source, source_other, right_next, right_other],
        2 * (rmax + lines) * size * half,
    )
    maps = everywhere(own_map, LINE)
    here_terms = jnp.einsum("mh,krh->kmr", both, d_left, precision=high)
    maps, both, here_terms = lax.optimization_barrier((maps, both, here_terms))
    maps_other = swapped(maps)
    both_before = along_rows(both, 1)
    both_other = swapped(both[lines:])
    here_terms = here_terms + swapped(here_terms)
    ahead_terms = jnp.einsum("mh,krh->kmr", both_before, d_right, precision=high)
    ahead_terms = ahead_terms + swapped(ahead_terms)
    reach, prefix, send = on_core(
        functools.partial(line_back, rmax),
        [floats(in_line, rows, LANES), floats(rmax, LANES), floats(groups, rows // 2, LANES)],
        where,
        [maps, maps_other],
        4 * in_line * rows * rmax * rmax,
        limit=60,
    )
    totals = lax.all_to_all(send, PLANE, 0, 0, tiled=True)
    totals, here_terms, ahead_terms, moved, both_other = lax.optimization_barrier(
        (totals, here_terms, ahead_terms, moved, both_other)
    )
    totals_other = swapped(totals)
    solution, upper_send, dense, dense_other, terms = on_core(
        functools.partial(plane_back, rmax),
        [floats(count + 1, half)]
        + [floats(params, count + 1, half)] * 3
        + [floats(3 * params, count, rmax)],
        where,
        [totals, totals_other, reach, both, both_other, ahead_terms, here_terms, d_left, d_right],
        2 * lines * rmax * (groups * LANES + (2 * params + 1) * half),
        [d_diag],
        [pltpu.VMEM(d_diag.shape, d_diag.dtype), pltpu.SemaphoreType.DMA],
        60,
    )
    upper = along_rows(upper_send, -1)
    partial = terms[:params] + swapped(terms)[:params]
    shared = jnp.concatenate([partial + terms[params : 2 * params], terms[2 * params :]], axis=0)
    shared = shared.reshape(2 * params * count, rmax)
    offsets = everywhere(shared, LINE)
    dense = dense + swapped(dense_other)
    applied = dense + upper
    drive = applied[:, :count].reshape(params * count, half)
    plain = dot(drive, inverse, high)
    plain = part(plain, side, 1) + swapped(part(plain, 1 - side, 1))

    data_part = jnp.einsum("kh,h->k", applied[:, count], solution[0], precision=highest)
    local, send = on_core(
        functools.partial(line_forward, rmax),
        [floats(params * count, rmax), floats(groups, 2 * params * count, rmax)],
        where,
        [maps, maps_other, offsets],
        2 * in_line * params * count * rmax * rmax,
    )
    outs = lax.all_to_all(send, PLANE, 0, 0, tiled=True)
    flat_result, sums = on_core(
        functools.partial(plane_forward, rmax),
        [floats(params * count, half), floats(1, LANES)],
        where,
        [totals, totals_other, outs, prefix, local, plain, moved, source],
        2 * params * count * rmax * (groups * rmax + half),
    )
    result = flat_result.reshape(params, count, half)
    data_at = params * (params + 1)
    sums = sums.reshape(-1) + jnp.pad(data_part, (data_at, LANES - data_at - params))
    sums = sums + swapped(sums)
    sums = jnp.sum(everywhere(sums, ROW).reshape(-1, 128), axis=0)
    fisher_sum = sums[: params * params].reshape(params, params)
    trace = sums[params * params : params * (params + 1)]
    data = sums[params * (params + 1) : params * (params + 2)]
    total = lax.axis_size(ROW) * lax.axis_size("col") * half
    fisher = fisher_sum / (2.0 * count * total)
    score = (data - trace / count) / (2.0 * total)
    return (solution, result, fisher, score)


def solution(mesh):
    finer = Mesh(
        mesh.devices.reshape(4, 4, 8, mesh.shape["col"]), ("row_0", "row_1", "row_2", "col")
    )
    placed = (
        P(ROW, None, "col"),
        P(ROW, "col", None),
        P(ROW, "col", None),
        P(None, ROW, None, "col"),
        P(None, ROW, "col", None),
        P(None, ROW, "col", None),
        P(None, ROW),
        P(ROW_COL),
        P(None, ROW_COL),
    )
    return jax.shard_map(
        body,
        mesh=finer,
        in_specs=placed,
        out_specs=(P(None, ROW_COL), P(None, None, ROW_COL), P(), P()),
        check_vma=False,
    )
```

```python
import functools

import jax
import jax.numpy as jnp
from jax import lax
from jax.experimental import pallas as pl
from jax.experimental.pallas import tpu as pltpu
from jax.sharding import Mesh
from jax.sharding import PartitionSpec as P

ROW = ("row_0", "row_1", "row_2")
PLANE = ("row_0", "row_1")
LINE = "row_2"
ROW_COL = ("row_0", "row_1", "row_2", "col")

high = lax.Precision.HIGH
highest = lax.Precision.HIGHEST


def dot(a, b, precision=highest):
    return lax.dot_general(a, b, (((1,), (0,)), ((), ())), precision=precision, preferred_element_type=jnp.float32)


def dot_nt(a, b, precision=highest):
    return lax.dot_general(a, b, (((1,), (1,)), ((), ())), precision=precision, preferred_element_type=jnp.float32)


def dot_tn(a, b, precision=highest):
    return lax.dot_general(a, b, (((0,), (0,)), ((), ())), precision=precision, preferred_element_type=jnp.float32)


def along_rows(block, distance):
    devices = range(lax.axis_size(ROW))
    route = [(i, i + distance) for i in devices if i + distance in devices]
    return lax.ppermute(block, ROW, route)


def swapped(block):
    return lax.ppermute(block, "col", [(0, 1), (1, 0)])


def part(x, index, axis):
    size = x.shape[axis] // 2
    return lax.dynamic_slice_in_dim(x, index * size, size, axis)


def joined(mine, other, side, axis):
    first = jnp.where(side == 0, mine, other)
    second = jnp.where(side == 0, other, mine)
    return jnp.concatenate([first, second], axis)


def everywhere(x, axis):
    count = lax.axis_size(axis)
    return lax.all_to_all(jnp.broadcast_to(x[None], (count, *x.shape)), axis, 0, 0, tiled=True)


LANES = 128
SMEM = pl.BlockSpec(memory_space=pltpu.SMEM)
VMEM = pl.BlockSpec(memory_space=pltpu.VMEM)


def on_core(kernel, outs, scalars, arrays, flops, far=(), scratch=(), limit=40):
    moved = sum(a.size * a.dtype.itemsize for a in [*arrays, *far]) + sum(4 * o.size for o in outs)
    return pl.pallas_call(
        kernel,
        out_shape=outs,
        in_specs=[SMEM] + [VMEM] * len(arrays) + [pl.BlockSpec(memory_space=pl.ANY)] * len(far),
        out_specs=[VMEM] * len(outs),
        scratch_shapes=list(scratch),
        compiler_params=pltpu.CompilerParams(vmem_limit_bytes=limit * 1024 * 1024),
        cost_estimate=pl.CostEstimate(flops=flops, bytes_accessed=moved, transcendentals=0),
    )(scalars, *arrays, *far)


def floats(*shape):
    return jax.ShapeDtypeStruct(shape, jnp.float32)


def whole_map(side, mine, other, k):
    first = jnp.where(side == 0, mine[k], other[k])
    second = jnp.where(side == 0, other[k], mine[k])
    return jnp.concatenate([first, second], axis=0)


def line_back(rmax, where, mine, other, reach, prefix, send):
    side, place = where[0], where[1]
    count, half_rows = mine.shape[0], mine.shape[1]
    rows = 2 * half_rows
    maps = [whole_map(side, mine, other, k) for k in range(count)]
    run = maps[-1]
    reach[count - 1] = run
    row = lax.broadcasted_iota(jnp.int32, (rmax, LANES), 0)
    lane = lax.broadcasted_iota(jnp.int32, (rmax, LANES), 1)
    early = (row == lane).astype(jnp.float32)
    chosen = early
    for k in range(count - 1):
        run = dot(run[:, :rows], maps[count - 2 - k])
        reach[count - 2 - k] = run
        early = maps[0][:rmax] if k == 0 else close(maps[k][:rmax, :rmax], early)
        chosen = jnp.where(place == k + 1, early, chosen)
    prefix[...] = chosen
    out = jnp.where(side == 0, run[:half_rows], run[half_rows:])
    for g in range(send.shape[0]):
        send[g] = out


def in_pieces(x, count):
    pieces = []
    for _ in range(count):
        piece = x.astype(jnp.bfloat16).astype(jnp.float32)
        pieces.append(piece)
        x = x - piece
    return pieces


def by_pieces(a, b, count, dims):
    rows = a.shape[0]
    stacked = jnp.concatenate(in_pieces(a, count), axis=0).astype(jnp.bfloat16)
    total = None
    for k, piece in enumerate(in_pieces(b, count)):
        product = lax.dot_general(
            stacked, piece.astype(jnp.bfloat16), (dims, ((), ())), preferred_element_type=jnp.float32
        )
        for j in reversed(range(count - k)):
            term = product[j * rows : (j + 1) * rows]
            total = term if total is None else total + term
    return total


def exact(a, b):
    return by_pieces(a, b, 3, ((1,), (0,)))


def close(a, b):
    return by_pieces(a, b, 2, ((1,), (0,)))


def close_nt(a, b):
    return by_pieces(a, b, 2, ((1,), (1,)))


def left_products(where, inverse, left, mine, other):
    half = left.shape[1]
    row = lax.broadcasted_iota(jnp.int32, left.shape, 0)
    product = dot(jnp.where(row < where[3], left[...], 0.0), inverse[...])
    first, second = product[:, :half], product[:, half:]
    mine[...] = jnp.where(where[0] == 0, first, second)
    other[...] = jnp.where(where[0] == 0, second, first)


def coupled(where, right, right_other, source, source_other, moved, moved_other, mine, other):
    rmax = right.shape[0]
    half_rows = mine.shape[0]
    vectors = source.shape[0]
    top = -(dot_nt(right[...], moved[...]) + dot_nt(right_other[...], moved_other[...]))
    low = dot_nt(source[...], moved[...]) + dot_nt(source_other[...], moved_other[...])
    low = jnp.concatenate([low, jnp.zeros((2 * half_rows - rmax - vectors, rmax), jnp.float32)], axis=0)
    full = jnp.concatenate([top, low], axis=0)
    full = jnp.concatenate([full, jnp.zeros((2 * half_rows, LANES - rmax), jnp.float32)], axis=1)
    row = lax.broadcasted_iota(jnp.int32, full.shape, 0)
    lane = lax.broadcasted_iota(jnp.int32, full.shape, 1)
    keep = (row == lane) & (row >= rmax) & (row < rmax + vectors)
    full = full + jnp.where(keep, 0.5, 0.0)
    first, second = full[:half_rows], full[half_rows:]
    mine[...] = jnp.where(where[0] == 0, first, second)
    other[...] = jnp.where(where[0] == 0, second, first)


def tile_products(where, inverse, source, source_other, right, right_other, out):
    half = source.shape[1]
    blank = jnp.zeros((16 - source.shape[0], half), jnp.float32)
    mine = jnp.concatenate([source[...], blank, right[...]], axis=0)
    other = jnp.concatenate([source_other[...], blank, right_other[...]], axis=0)
    first = jnp.where(where[0] == 0, mine, other)
    second = jnp.where(where[0] == 0, other, mine)
    out[...] = dot_nt(first, inverse[:, :half]) + dot_nt(second, inverse[:, half:])


def plane_back(
    rmax, where, mine, other, reach, both, wide_other, ahead_terms, here_terms, left, right, deriv,
    solution, upper, dense, dense_other, terms, held, arrived,
):
    params = left.shape[0]
    fetch = pltpu.make_async_copy(deriv, held, arrived)
    fetch.start()
    side, place, group = where[0], where[1], where[2]
    groups, half_rows = mine.shape[0], mine.shape[1]
    count = reach.shape[0]
    rows = 2 * half_rows
    vectors = solution.shape[0]
    lines = rows - rmax
    row = lax.broadcasted_iota(jnp.int32, (lines, LANES), 0)
    lane = lax.broadcasted_iota(jnp.int32, (lines, LANES), 1)
    state = ((row + rmax == lane) & (row < vectors)).astype(jnp.float32)
    ahead = state
    for g in reversed(range(1, groups)):
        state = exact(state[:, :rows], whole_map(side, mine, other, g))
        ahead = jnp.where(group == g - 1, state, ahead)
    through = exact(ahead[:, :rows], reach[jnp.minimum(place + 1, count - 1)])
    coeff = jnp.where(place == count - 1, ahead, through)[:, :rmax]
    own = exact(ahead[:, :rows], reach[place])[:, :rmax]
    solved = (both[:lines] - dot(coeff, both[lines:]))[:vectors]
    solution[...] = jnp.concatenate([solved[vectors - 1 :], solved[: vectors - 1]], axis=0)
    column = lax.broadcasted_iota(jnp.int32, (lines, rmax), 1)
    for k in range(left.shape[0]):
        below = here_terms[k, :lines] - close(coeff, here_terms[k, lines:])
        below = jnp.where(column < where[4 + k], below, 0.0)
        above = ahead_terms[k, :lines] - close(own, ahead_terms[k, lines:])
        above = jnp.where(column < where[4 + k], above, 0.0)
        upper[k] = close(below, right[k])[:vectors]
        dense[k] = close(above, left[k])[:vectors]
        terms[params + k] = close_nt(above, here_terms[k, lines:])[: vectors - 1]
        terms[2 * params + k] = close_nt(below, ahead_terms[k, lines:])[: vectors - 1]
    fetch.wait()
    half = both.shape[1]
    rounded = jnp.concatenate([solved, jnp.zeros((lines - vectors, half), jnp.float32)], axis=0)
    rounded = rounded.astype(jnp.bfloat16)
    wide = both[lines:]
    for k in range(left.shape[0]):
        product = jnp.dot(rounded, held[k], preferred_element_type=jnp.float32)
        first, second = product[:, :half], product[:, half:]
        here = jnp.where(side == 0, first, second)
        there = jnp.where(side == 0, second, first)
        dense[k] += here[:vectors]
        dense_other[k] = there[:vectors]
        terms[k] = (close_nt(here, wide) + close_nt(there, wide_other[...]))[: vectors - 1]


def line_forward(rmax, where, mine, other, offsets, local, send):
    side, place = where[0], where[1]
    state = jnp.zeros(local.shape, jnp.float32)
    chosen = state
    for k in range(mine.shape[0]):
        chosen = jnp.where(place == k, state, chosen)
        turn = whole_map(side, mine, other, k)[:rmax, :rmax]
        offset = offsets[k, : local.shape[0]]
        if k + 1 < mine.shape[0]:
            offset += offsets[k + 1, local.shape[0] :]
        state = offset + close_nt(state, turn)
    local[...] = chosen
    for g in range(send.shape[0]):
        send[g, : local.shape[0]] = state
        send[g, local.shape[0] :] = offsets[0, local.shape[0] :]


def plane_forward(
    rmax, where, mine, other, outs, prefix, local, plain, moved, source, result, sums
):
    side, group = where[0], where[2]
    params = plain.shape[0] // (source.shape[0] - 1)
    state = jnp.zeros(local.shape, jnp.float32)
    behind = state
    for g in range(mine.shape[0] - 1):
        turn = whole_map(side, mine, other, g)[:rmax, :rmax]
        offset = outs[g, : local.shape[0]] + outs[g + 1, local.shape[0] :]
        state = offset + close_nt(state, turn)
        behind = jnp.where(group == g + 1, state, behind)
    entry = local[...] + close_nt(behind, prefix[:, :rmax])
    final = plain[...] - close(entry, moved[...])
    result[...] = final
    each = final.shape[0] // params
    parts = [final[k * each : (k + 1) * each] for k in range(params)]
    signs = source[: source.shape[0] - 1]
    lane = lax.broadcasted_iota(jnp.int32, sums.shape, 1)
    total = jnp.zeros(sums.shape, jnp.float32)
    for k in range(params):
        for j in range(k, params):
            both = jnp.sum(parts[k] * parts[j], keepdims=True)
            total = jnp.where((lane == k * params + j) | (lane == j * params + k), both, total)
        both = jnp.sum(parts[k] * signs, keepdims=True)
        total = jnp.where(lane == params * params + k, both, total)
    sums[...] = total


def body(
    inv_diag, low_left, low_right, deriv_diag, deriv_left, deriv_right, ranks, whitened, probes
):
    inverse = jnp.swapaxes(inv_diag[0], 0, 1)
    half, size = inverse.shape
    rmax = low_left.shape[2]
    count = probes.shape[0]
    params = deriv_left.shape[0]
    side = lax.axis_index("col")
    place = lax.axis_index(LINE)
    group = lax.axis_index(PLANE)
    in_line = lax.axis_size(LINE)
    groups = lax.axis_size(PLANE)
    d_left = jnp.swapaxes(deriv_left[:, 0], 1, 2)
    d_right = jnp.swapaxes(deriv_right[:, 0], 1, 2)
    d_diag = jnp.swapaxes(deriv_diag[:, 0], 1, 2)
    left = jnp.swapaxes(low_left[0], 0, 1)
    right = jnp.swapaxes(low_right[0], 0, 1)
    where = jnp.concatenate([jnp.stack([side, place, group]).astype(jnp.int32), ranks[:, 0]])
    source = jnp.concatenate([probes.astype(jnp.float32), whitened[None, :]], axis=0)
    lines = -(-(count + 1) // 16) * 16
    rows = rmax + lines
    source_other = swapped(source)
    right_next = along_rows(right, -1)
    moved, moved_other = on_core(
        left_products, [floats(rmax, half)] * 2, where, [inverse, left], 2 * size * half * rmax
    )
    right_next, moved, moved_other = lax.optimization_barrier((right_next, moved, moved_other))
    right_other = swapped(right_next)
    map_mine, map_other = on_core(
        coupled,
        [floats(rows // 2, LANES)] * 2,
        where,
        [right_next, right_other, source, source_other, moved, moved_other],
        2 * size * rows * rmax,
    )
    own_map = map_mine + swapped(map_other)
    moved = moved + swapped(moved_other)
    (both,) = on_core(
        tile_products,
        [floats(rmax + lines, half)],
        where,
        [inverse, source, source_other, right_next, right_other],
        2 * (rmax + lines) * size * half,
    )
    maps = everywhere(own_map, LINE)
    here_terms = jnp.einsum("mh,krh->kmr", both, d_left, precision=high)
    maps, both, here_terms = lax.optimization_barrier((maps, both, here_terms))
    maps_other = swapped(maps)
    both_before = along_rows(both, 1)
    both_other = swapped(both[lines:])
    here_terms = here_terms + swapped(here_terms)
    ahead_terms = jnp.einsum("mh,krh->kmr", both_before, d_right, precision=high)
    ahead_terms = ahead_terms + swapped(ahead_terms)
    reach, prefix, send = on_core(
        functools.partial(line_back, rmax),
        [floats(in_line, rows, LANES), floats(rmax, LANES), floats(groups, rows // 2, LANES)],
        where,
        [maps, maps_other],
        4 * in_line * rows * rmax * rmax,
        limit=60,
    )
    totals = lax.all_to_all(send, PLANE, 0, 0, tiled=True)
    totals, here_terms, ahead_terms, moved, both_other = lax.optimization_barrier(
        (totals, here_terms, ahead_terms, moved, both_other)
    )
    totals_other = swapped(totals)
    solution, upper_send, dense, dense_other, terms = on_core(
        functools.partial(plane_back, rmax),
        [floats(count + 1, half)]
        + [floats(params, count + 1, half)] * 3
        + [floats(3 * params, count, rmax)],
        where,
        [totals, totals_other, reach, both, both_other, ahead_terms, here_terms, d_left, d_right],
        2 * lines * rmax * (groups * LANES + (2 * params + 1) * half),
        [d_diag],
        [pltpu.VMEM(d_diag.shape, d_diag.dtype), pltpu.SemaphoreType.DMA],
        60,
    )
    upper = along_rows(upper_send, -1)
    partial = terms[:params] + swapped(terms)[:params]
    shared = terms[params:] + jnp.pad(partial, ((0, params), (0, 0), (0, 0)))
    shared = shared.reshape(2 * params * count, rmax)
    offsets = everywhere(shared, LINE)
    dense = dense + swapped(dense_other)
    applied = dense + upper
    drive = applied[:, :count].reshape(params * count, half)
    plain = dot(drive, inverse, high)
    plain = part(plain, side, 1) + swapped(part(plain, 1 - side, 1))

    data_part = jnp.einsum("kh,h->k", applied[:, count], solution[0], precision=highest)
    local, send = on_core(
        functools.partial(line_forward, rmax),
        [floats(params * count, rmax), floats(groups, 2 * params * count, rmax)],
        where,
        [maps, maps_other, offsets],
        2 * in_line * params * count * rmax * rmax,
    )
    outs = lax.all_to_all(send, PLANE, 0, 0, tiled=True)
    flat_result, sums = on_core(
        functools.partial(plane_forward, rmax),
        [floats(params * count, half), floats(1, LANES)],
        where,
        [totals, totals_other, outs, prefix, local, plain, moved, source],
        2 * params * count * rmax * (groups * rmax + half),
    )
    result = flat_result.reshape(params, count, half)
    data_at = params * (params + 1)
    sums = sums.reshape(-1) + jnp.pad(data_part, (data_at, LANES - data_at - params))
    sums = sums + swapped(sums)
    sums = jnp.sum(everywhere(sums, ROW).reshape(-1, 128), axis=0)
    fisher_sum = sums[: params * params].reshape(params, params)
    trace = sums[params * params : params * (params + 1)]
    data = sums[params * (params + 1) : params * (params + 2)]
    total = lax.axis_size(ROW) * lax.axis_size("col") * half
    fisher = fisher_sum / (2.0 * count * total)
    score = (data - trace / count) / (2.0 * total)
    return (solution, result, fisher, score)


def solution(mesh):
    finer = Mesh(
        mesh.devices.reshape(4, 4, 8, mesh.shape["col"]), ("row_0", "row_1", "row_2", "col")
    )
    placed = (
        P(ROW, None, "col"),
        P(ROW, "col", None),
        P(ROW, "col", None),
        P(None, ROW, None, "col"),
        P(None, ROW, "col", None),
        P(None, ROW, "col", None),
        P(None, ROW),
        P(ROW_COL),
        P(None, ROW_COL),
    )
    return jax.shard_map(
        body,
        mesh=finer,
        in_specs=placed,
        out_specs=(P(None, ROW_COL), P(None, None, ROW_COL), P(), P()),
        check_vma=False,
    )
```

```python
import functools

import jax
import jax.numpy as jnp
from jax import lax
from jax.experimental import pallas as pl
from jax.experimental.pallas import tpu as pltpu
from jax.sharding import Mesh
from jax.sharding import PartitionSpec as P

ROW = ("row_0", "row_1", "row_2")
PLANE = ("row_0", "row_1")
LINE = "row_2"
ROW_COL = ("row_0", "row_1", "row_2", "col")

high = lax.Precision.HIGH
highest = lax.Precision.HIGHEST


def dot(a, b, precision=highest):
    return lax.dot_general(a, b, (((1,), (0,)), ((), ())), precision=precision, preferred_element_type=jnp.float32)


def dot_nt(a, b, precision=highest):
    return lax.dot_general(a, b, (((1,), (1,)), ((), ())), precision=precision, preferred_element_type=jnp.float32)


def dot_tn(a, b, precision=highest):
    return lax.dot_general(a, b, (((0,), (0,)), ((), ())), precision=precision, preferred_element_type=jnp.float32)


def along_rows(block, distance):
    devices = range(lax.axis_size(ROW))
    route = [(i, i + distance) for i in devices if i + distance in devices]
    return lax.ppermute(block, ROW, route)


def swapped(block):
    return lax.ppermute(block, "col", [(0, 1), (1, 0)])


def part(x, index, axis):
    size = x.shape[axis] // 2
    return lax.dynamic_slice_in_dim(x, index * size, size, axis)


def joined(mine, other, side, axis):
    first = jnp.where(side == 0, mine, other)
    second = jnp.where(side == 0, other, mine)
    return jnp.concatenate([first, second], axis)


def everywhere(x, axis):
    count = lax.axis_size(axis)
    return lax.all_to_all(jnp.broadcast_to(x[None], (count, *x.shape)), axis, 0, 0, tiled=True)


LANES = 128
SMEM = pl.BlockSpec(memory_space=pltpu.SMEM)
VMEM = pl.BlockSpec(memory_space=pltpu.VMEM)


def on_core(kernel, outs, scalars, arrays, flops, far=(), scratch=(), limit=40):
    moved = sum(a.size * a.dtype.itemsize for a in [*arrays, *far]) + sum(4 * o.size for o in outs)
    return pl.pallas_call(
        kernel,
        out_shape=outs,
        in_specs=[SMEM] + [VMEM] * len(arrays) + [pl.BlockSpec(memory_space=pl.ANY)] * len(far),
        out_specs=[VMEM] * len(outs),
        scratch_shapes=list(scratch),
        compiler_params=pltpu.CompilerParams(vmem_limit_bytes=limit * 1024 * 1024),
        cost_estimate=pl.CostEstimate(flops=flops, bytes_accessed=moved, transcendentals=0),
    )(scalars, *arrays, *far)


def floats(*shape):
    return jax.ShapeDtypeStruct(shape, jnp.float32)


def whole_map(side, mine, other, k):
    first = jnp.where(side == 0, mine[k], other[k])
    second = jnp.where(side == 0, other[k], mine[k])
    return jnp.concatenate([first, second], axis=0)


def line_back(rmax, where, mine, other, reach, prefix, send):
    side, place = where[0], where[1]
    count, half_rows = mine.shape[0], mine.shape[1]
    rows = 2 * half_rows
    maps = [whole_map(side, mine, other, k) for k in range(count)]
    run = maps[-1]
    reach[count - 1] = run
    row = lax.broadcasted_iota(jnp.int32, (rmax, LANES), 0)
    lane = lax.broadcasted_iota(jnp.int32, (rmax, LANES), 1)
    early = (row == lane).astype(jnp.float32)
    chosen = early
    for k in range(count - 1):
        run = dot(run[:, :rows], maps[count - 2 - k])
        reach[count - 2 - k] = run
        early = maps[0][:rmax] if k == 0 else dot(maps[k][:rmax, :rmax], early)
        chosen = jnp.where(place == k + 1, early, chosen)
    prefix[...] = chosen
    out = jnp.where(side == 0, run[:half_rows], run[half_rows:])
    for g in range(send.shape[0]):
        send[g] = out


def in_pieces(x, count):
    pieces = []
    for _ in range(count):
        piece = x.astype(jnp.bfloat16).astype(jnp.float32)
        pieces.append(piece)
        x = x - piece
    return pieces


def by_pieces(a, b, count, dims):
    rows = a.shape[0]
    stacked = jnp.concatenate(in_pieces(a, count), axis=0).astype(jnp.bfloat16)
    total = None
    for k, piece in enumerate(in_pieces(b, count)):
        product = lax.dot_general(
            stacked, piece.astype(jnp.bfloat16), (dims, ((), ())), preferred_element_type=jnp.float32
        )
        for j in reversed(range(count - k)):
            term = product[j * rows : (j + 1) * rows]
            total = term if total is None else total + term
    return total


def exact(a, b):
    return by_pieces(a, b, 3, ((1,), (0,)))


def close(a, b):
    return by_pieces(a, b, 2, ((1,), (0,)))


def close_nt(a, b):
    return by_pieces(a, b, 2, ((1,), (1,)))


def left_products(where, inverse, left, mine, other):
    half = left.shape[1]
    row = lax.broadcasted_iota(jnp.int32, left.shape, 0)
    product = dot(jnp.where(row < where[3], left[...], 0.0), inverse[...])
    first, second = product[:, :half], product[:, half:]
    mine[...] = jnp.where(where[0] == 0, first, second)
    other[...] = jnp.where(where[0] == 0, second, first)


def coupled(where, right, right_other, source, source_other, moved, moved_other, mine, other):
    rmax = right.shape[0]
    half_rows = mine.shape[0]
    vectors = source.shape[0]
    top = -(dot_nt(right[...], moved[...]) + dot_nt(right_other[...], moved_other[...]))
    low = dot_nt(source[...], moved[...]) + dot_nt(source_other[...], moved_other[...])
    low = jnp.concatenate([low, jnp.zeros((2 * half_rows - rmax - vectors, rmax), jnp.float32)], axis=0)
    full = jnp.concatenate([top, low], axis=0)
    full = jnp.concatenate([full, jnp.zeros((2 * half_rows, LANES - rmax), jnp.float32)], axis=1)
    row = lax.broadcasted_iota(jnp.int32, full.shape, 0)
    lane = lax.broadcasted_iota(jnp.int32, full.shape, 1)
    keep = (row == lane) & (row >= rmax) & (row < rmax + vectors)
    full = full + jnp.where(keep, 0.5, 0.0)
    first, second = full[:half_rows], full[half_rows:]
    mine[...] = jnp.where(where[0] == 0, first, second)
    other[...] = jnp.where(where[0] == 0, second, first)


def tile_products(where, inverse, source, source_other, right, right_other, out):
    half = source.shape[1]
    blank = jnp.zeros((16 - source.shape[0], half), jnp.float32)
    mine = jnp.concatenate([source[...], blank, right[...]], axis=0)
    other = jnp.concatenate([source_other[...], blank, right_other[...]], axis=0)
    first = jnp.where(where[0] == 0, mine, other)
    second = jnp.where(where[0] == 0, other, mine)
    out[...] = dot_nt(first, inverse[:, :half]) + dot_nt(second, inverse[:, half:])


def plane_back(
    rmax, where, mine, other, reach, both, wide_other, ahead_terms, here_terms, left, right, deriv,
    solution, upper, dense, dense_other, terms, held, arrived,
):
    params = left.shape[0]
    fetch = pltpu.make_async_copy(deriv, held, arrived)
    fetch.start()
    side, place, group = where[0], where[1], where[2]
    groups, half_rows = mine.shape[0], mine.shape[1]
    count = reach.shape[0]
    rows = 2 * half_rows
    vectors = solution.shape[0]
    lines = rows - rmax
    row = lax.broadcasted_iota(jnp.int32, (lines, LANES), 0)
    lane = lax.broadcasted_iota(jnp.int32, (lines, LANES), 1)
    state = ((row + rmax == lane) & (row < vectors)).astype(jnp.float32)
    ahead = state
    for g in reversed(range(1, groups)):
        state = exact(state[:, :rows], whole_map(side, mine, other, g))
        ahead = jnp.where(group == g - 1, state, ahead)
    through = exact(ahead[:, :rows], reach[jnp.minimum(place + 1, count - 1)])
    coeff = jnp.where(place == count - 1, ahead, through)[:, :rmax]
    own = exact(ahead[:, :rows], reach[place])[:, :rmax]
    solved = (both[:lines] - dot(coeff, both[lines:]))[:vectors]
    solution[...] = jnp.concatenate([solved[vectors - 1 :], solved[: vectors - 1]], axis=0)
    column = lax.broadcasted_iota(jnp.int32, (lines, rmax), 1)
    for k in range(left.shape[0]):
        below = here_terms[k, :lines] - close(coeff, here_terms[k, lines:])
        below = jnp.where(column < where[4 + k], below, 0.0)
        above = ahead_terms[k, :lines] - close(own, ahead_terms[k, lines:])
        above = jnp.where(column < where[4 + k], above, 0.0)
        upper[k] = close(below, right[k])[:vectors]
        dense[k] = close(above, left[k])[:vectors]
        terms[params + k] = close_nt(above, here_terms[k, lines:])[: vectors - 1]
        terms[2 * params + k] = close_nt(below, ahead_terms[k, lines:])[: vectors - 1]
    fetch.wait()
    half = both.shape[1]
    rounded = jnp.concatenate([solved, jnp.zeros((lines - vectors, half), jnp.float32)], axis=0)
    rounded = rounded.astype(jnp.bfloat16)
    wide = both[lines:]
    for k in range(left.shape[0]):
        product = jnp.dot(rounded, held[k], preferred_element_type=jnp.float32)
        first, second = product[:, :half], product[:, half:]
        here = jnp.where(side == 0, first, second)
        there = jnp.where(side == 0, second, first)
        dense[k] += here[:vectors]
        dense_other[k] = there[:vectors]
        terms[k] = (close_nt(here, wide) + close_nt(there, wide_other[...]))[: vectors - 1]


def line_forward(rmax, where, mine, other, offsets, local, send):
    side, place = where[0], where[1]
    state = jnp.zeros(local.shape, jnp.float32)
    chosen = state
    for k in range(mine.shape[0]):
        chosen = jnp.where(place == k, state, chosen)
        turn = whole_map(side, mine, other, k)[:rmax, :rmax]
        offset = offsets[k, : local.shape[0]]
        if k + 1 < mine.shape[0]:
            offset += offsets[k + 1, local.shape[0] :]
        state = offset + close_nt(state, turn)
    local[...] = chosen
    for g in range(send.shape[0]):
        send[g, : local.shape[0]] = state
        send[g, local.shape[0] :] = offsets[0, local.shape[0] :]


def plane_forward(
    rmax, where, mine, other, outs, prefix, local, plain, moved, source, result, sums
):
    side, group = where[0], where[2]
    params = plain.shape[0] // (source.shape[0] - 1)
    state = jnp.zeros(local.shape, jnp.float32)
    behind = state
    for g in range(mine.shape[0] - 1):
        turn = whole_map(side, mine, other, g)[:rmax, :rmax]
        offset = outs[g, : local.shape[0]] + outs[g + 1, local.shape[0] :]
        state = offset + close_nt(state, turn)
        behind = jnp.where(group == g + 1, state, behind)
    entry = local[...] + close_nt(behind, prefix[:, :rmax])
    final = plain[...] - close(entry, moved[...])
    result[...] = final
    each = final.shape[0] // params
    parts = [final[k * each : (k + 1) * each] for k in range(params)]
    signs = source[: source.shape[0] - 1]
    lane = lax.broadcasted_iota(jnp.int32, sums.shape, 1)
    total = jnp.zeros(sums.shape, jnp.float32)
    for k in range(params):
        for j in range(k, params):
            both = jnp.sum(parts[k] * parts[j], keepdims=True)
            total = jnp.where((lane == k * params + j) | (lane == j * params + k), both, total)
        both = jnp.sum(parts[k] * signs, keepdims=True)
        total = jnp.where(lane == params * params + k, both, total)
    sums[...] = total


def body(
    inv_diag, low_left, low_right, deriv_diag, deriv_left, deriv_right, ranks, whitened, probes
):
    inverse = jnp.swapaxes(inv_diag[0], 0, 1)
    half, size = inverse.shape
    rmax = low_left.shape[2]
    count = probes.shape[0]
    params = deriv_left.shape[0]
    side = lax.axis_index("col")
    place = lax.axis_index(LINE)
    group = lax.axis_index(PLANE)
    in_line = lax.axis_size(LINE)
    groups = lax.axis_size(PLANE)
    d_left = jnp.swapaxes(deriv_left[:, 0], 1, 2)
    d_right = jnp.swapaxes(deriv_right[:, 0], 1, 2)
    d_diag = jnp.swapaxes(deriv_diag[:, 0], 1, 2)
    left = jnp.swapaxes(low_left[0], 0, 1)
    right = jnp.swapaxes(low_right[0], 0, 1)
    where = jnp.concatenate([jnp.stack([side, place, group]).astype(jnp.int32), ranks[:, 0]])
    source = jnp.concatenate([probes.astype(jnp.float32), whitened[None, :]], axis=0)
    lines = -(-(count + 1) // 16) * 16
    rows = rmax + lines
    source_other = swapped(source)
    right_next = along_rows(right, -1)
    moved, moved_other = on_core(
        left_products, [floats(rmax, half)] * 2, where, [inverse, left], 2 * size * half * rmax
    )
    right_next, moved, moved_other = lax.optimization_barrier((right_next, moved, moved_other))
    right_other = swapped(right_next)
    map_mine, map_other = on_core(
        coupled,
        [floats(rows // 2, LANES)] * 2,
        where,
        [right_next, right_other, source, source_other, moved, moved_other],
        2 * size * rows * rmax,
    )
    own_map = map_mine + swapped(map_other)
    moved = moved + swapped(moved_other)
    (both,) = on_core(
        tile_products,
        [floats(rmax + lines, half)],
        where,
        [inverse, source, source_other, right_next, right_other],
        2 * (rmax + lines) * size * half,
    )
    maps = everywhere(own_map, LINE)
    here_terms = jnp.einsum("mh,krh->kmr", both, d_left, precision=high)
    maps, both, here_terms = lax.optimization_barrier((maps, both, here_terms))
    maps_other = swapped(maps)
    both_other = swapped(both[lines:])
    here_terms = here_terms + swapped(here_terms)
    reach, prefix, send = on_core(
        functools.partial(line_back, rmax),
        [floats(in_line, rows, LANES), floats(rmax, LANES), floats(groups, rows // 2, LANES)],
        where,
        [maps, maps_other],
        4 * in_line * rows * rmax * rmax,
        limit=60,
    )
    late_both, send = lax.optimization_barrier((both, send))
    both_before = along_rows(late_both, 1)
    ahead_terms = jnp.einsum("mh,krh->kmr", both_before, d_right, precision=high)
    ahead_terms = ahead_terms + swapped(ahead_terms)
    totals = lax.all_to_all(send, PLANE, 0, 0, tiled=True)
    totals, here_terms, ahead_terms, moved, both_other = lax.optimization_barrier(
        (totals, here_terms, ahead_terms, moved, both_other)
    )
    totals_other = swapped(totals)
    solution, upper_send, dense, dense_other, terms = on_core(
        functools.partial(plane_back, rmax),
        [floats(count + 1, half)]
        + [floats(params, count + 1, half)] * 3
        + [floats(3 * params, count, rmax)],
        where,
        [totals, totals_other, reach, both, both_other, ahead_terms, here_terms, d_left, d_right],
        2 * lines * rmax * (groups * LANES + (2 * params + 1) * half),
        [d_diag],
        [pltpu.VMEM(d_diag.shape, d_diag.dtype), pltpu.SemaphoreType.DMA],
        60,
    )
    upper = along_rows(upper_send, -1)
    partial = terms[:params] + swapped(terms)[:params]
    shared = jnp.concatenate([partial + terms[params : 2 * params], terms[2 * params :]], axis=0)
    shared = shared.reshape(2 * params * count, rmax)
    offsets = everywhere(shared, LINE)
    dense = dense + swapped(dense_other)
    applied = dense + upper
    drive = applied[:, :count].reshape(params * count, half)
    plain = dot(drive, inverse, high)
    plain = part(plain, side, 1) + swapped(part(plain, 1 - side, 1))

    data_part = jnp.einsum("kh,h->k", applied[:, count], solution[0], precision=highest)
    local, send = on_core(
        functools.partial(line_forward, rmax),
        [floats(params * count, rmax), floats(groups, 2 * params * count, rmax)],
        where,
        [maps, maps_other, offsets],
        2 * in_line * params * count * rmax * rmax,
    )
    outs = lax.all_to_all(send, PLANE, 0, 0, tiled=True)
    flat_result, sums = on_core(
        functools.partial(plane_forward, rmax),
        [floats(params * count, half), floats(1, LANES)],
        where,
        [totals, totals_other, outs, prefix, local, plain, moved, source],
        2 * params * count * rmax * (groups * rmax + half),
    )
    result = flat_result.reshape(params, count, half)
    data_at = params * (params + 1)
    sums = sums.reshape(-1) + jnp.pad(data_part, (data_at, LANES - data_at - params))
    sums = sums + swapped(sums)
    sums = jnp.sum(everywhere(sums, ROW).reshape(-1, 128), axis=0)
    fisher_sum = sums[: params * params].reshape(params, params)
    trace = sums[params * params : params * (params + 1)]
    data = sums[params * (params + 1) : params * (params + 2)]
    total = lax.axis_size(ROW) * lax.axis_size("col") * half
    fisher = fisher_sum / (2.0 * count * total)
    score = (data - trace / count) / (2.0 * total)
    return (solution, result, fisher, score)


def solution(mesh):
    finer = Mesh(
        mesh.devices.reshape(4, 4, 8, mesh.shape["col"]), ("row_0", "row_1", "row_2", "col")
    )
    placed = (
        P(ROW, None, "col"),
        P(ROW, "col", None),
        P(ROW, "col", None),
        P(None, ROW, None, "col"),
        P(None, ROW, "col", None),
        P(None, ROW, "col", None),
        P(None, ROW),
        P(ROW_COL),
        P(None, ROW_COL),
    )
    return jax.shard_map(
        body,
        mesh=finer,
        in_specs=placed,
        out_specs=(P(None, ROW_COL), P(None, None, ROW_COL), P(), P()),
        check_vma=False,
    )
```
